32 devices in a mesh: section: 2 (over y), seq: 16 (over z, x, core).
Axes of the slice: x: 2, y: 2, z: 4, core: 2. Of those that a mesh axis runs over, the one named last changes fastest.
Arguments:
- resident_microbatches: bfloat16 [2, 2048, 1024], P('section', 'seq'), may hold values from -64 to 64
- arriving_microbatch: bfloat16 [2048, 1024], P('seq'), may hold values from -64 to 64
- prenormal_scaling: float32 [2, 1024], P('section'), may hold values from 0.1 to 1.9
- attention_triple_matrix: bfloat16 [2, 1024, 3072], P('section', 'seq'), may hold values from -0.1875 to 0.1875
- exit_projection_matrix: bfloat16 [2, 1024, 1024], P('section'), may hold values from -0.1875 to 0.1875
- mirrored_lookup_tile: int32 [16, 4], replicated, may hold values from 0 to 1
Outputs:
- tick_out: bfloat16 [2, 2, 2048, 1024], P(None, 'section', 'seq')
The draws below stay inside these ranges and needn't reach their ends.
All inputs are finite; a program needn't handle non-finite values.
Results may differ from the reference program's by a relative error of at most 0.004.
Values may be sent and summed in bfloat16 or wider, within the bound.
No kernel may reach another device: no remote copies, remote signals or barrier semaphores. Data moves between devices by JAX's collectives and lax.ppermute only.
A program may use at most 64 MiB of HBM per device.

```python
import math
import jax
import jax.numpy as jnp
from jax import lax

D = 1024
HEADS = 8
HEAD = 128
BLOCK = 64
LEVELS = 4
TOK_DEV = 128
INNER = 1024
BLK_DEV = 2
TOKENS = 2048
SECTIONS = 2
N_SEQ = 16


def scaled_field(key, lead, row_count, col_count):
    first_key, second_key, third_key = jax.random.split(key, 3)
    log_low = math.log(0.3)
    log_high = math.log(3.0)
    col_scale = jnp.exp(jax.random.uniform(first_key, (lead, 1, col_count), jnp.float32, log_low, log_high))
    row_scale = jnp.exp(jax.random.uniform(second_key, (lead, row_count, 1), jnp.float32, log_low, log_high))
    base = jnp.clip(jax.random.normal(third_key, (lead, row_count, col_count), jnp.float32), -6.0, 6.0)
    return base * row_scale * col_scale


def draw_resident_microbatches(key, part):
    return scaled_field(jax.random.fold_in(key, 11), SECTIONS, TOKENS, D).astype(jnp.bfloat16)


def draw_arriving_microbatch(key, part):
    return scaled_field(jax.random.fold_in(key, 23), 1, TOKENS, D)[0].astype(jnp.bfloat16)


def place_ends(values, stream_key, least, top_value):
    spot = [jax.random.randint(jax.random.fold_in(stream_key, axis), (), 0, length) for axis, length in enumerate(values.shape)]
    main_axis = values.shape.index(max(values.shape))
    beside = spot[:main_axis] + [(spot[main_axis] + 1) % values.shape[main_axis]] + spot[main_axis + 1:]
    return values.at[tuple(spot)].set(least).at[tuple(beside)].set(top_value)


def levels(rng, shape, pieces, smallest, high):
    def one(dim, shards_of):
        heights = jax.random.uniform(jax.random.fold_in(jax.random.fold_in(rng, 6), dim), (shards_of,), jnp.float32, smallest / len(pieces), high / len(pieces))
        return jnp.repeat(jnp.exp(heights), shape[dim] // shards_of).reshape((-1,) + (1,) * (len(shape) - dim - 1))

    loudness = one(*pieces[0])
    for cut in pieces[1:]:
        loudness = loudness * one(*cut)
    return loudness


def scatter_about(stream_key, extent, scale, bound, pieces=(), held_as=jnp.bfloat16):
    entries = scale * jax.random.normal(stream_key, extent, jnp.float32)
    if pieces:
        entries = entries * levels(stream_key, extent, pieces, -0.22, 0.18)
    return jnp.clip(entries, -bound, bound).astype(held_as)


def setup_inputs(seed: int = 0) -> dict:
    key_list = jax.random.split(jax.random.key(seed), 7)
    return {
        "resident_microbatches": draw_resident_microbatches(jax.random.fold_in(key_list[6], 71), 0),
        "arriving_microbatch": draw_arriving_microbatch(jax.random.fold_in(key_list[6], 71), 0),
        "prenormal_scaling": jnp.clip(1.0 + 0.18 * jax.random.normal(key_list[2], (SECTIONS, D), jnp.float32), 0.1, 1.9),
        "attention_triple_matrix": scatter_about(key_list[3], (SECTIONS, D, 3 * INNER), D ** -0.5, 0.1875, ((0, 2), (1, 16))),
        "exit_projection_matrix": scatter_about(key_list[4], (SECTIONS, INNER, D), INNER ** -0.5, 0.1875, ((0, 2),)),
        "mirrored_lookup_tile": place_ends(jax.random.randint(key_list[5], (N_SEQ, LEVELS), 0, BLK_DEV), jax.random.fold_in(key_list[5], 1), 0, BLK_DEV - 1).astype(jnp.int32),
    }


epsilon = 1e-06

def head_norm(projected, row_count):
    shaped = projected.reshape(row_count, HEADS, HEAD)
    mean_square = lax.optimization_barrier(jnp.mean(shaped * shaped, axis=-1, keepdims=True))
    return (shaped * lax.rsqrt(mean_square + epsilon)).astype(jnp.bfloat16)

def attend_device(operands):
    queries, own_keys, own_values, far_keys, far_values = operands
    blocks = queries.shape[0]
    score_scale = HEAD ** (-0.5)
    far_keys = jnp.broadcast_to(far_keys.reshape(1, LEVELS * BLOCK, HEADS, HEAD), (blocks, LEVELS * BLOCK, HEADS, HEAD))
    far_values = jnp.broadcast_to(far_values.reshape(1, LEVELS * BLOCK, HEADS, HEAD), (blocks, LEVELS * BLOCK, HEADS, HEAD))
    all_keys = jnp.concatenate([own_keys, far_keys], axis=1)
    all_values = jnp.concatenate([own_values, far_values], axis=1)
    scores = jnp.einsum('cqhd,ckhd->chqk', queries.astype(jnp.float32), all_keys.astype(jnp.float32)) * score_scale
    exps = jnp.exp(scores)
    weights = (exps / lax.optimization_barrier(jnp.sum(exps, axis=-1, keepdims=True))).astype(jnp.bfloat16)
    mixed_heads = jnp.einsum('chqk,ckhd->cqhd', weights.astype(jnp.float32), all_values.astype(jnp.float32))
    return mixed_heads.astype(jnp.bfloat16)

def transform_through_tier(hidden_in, gain_row, weights, out_weights, mirrored_lookup_tile):
    inner_width = HEADS * HEAD
    blocks = TOK_DEV // BLOCK
    widened = hidden_in.astype(jnp.float32)
    mean_square = lax.optimization_barrier(jnp.mean(widened * widened, axis=-1, keepdims=True))
    normed = (widened * lax.rsqrt(mean_square + epsilon) * gain_row.astype(jnp.float32)).astype(jnp.bfloat16)
    projected = jnp.dot(normed, weights, preferred_element_type=jnp.float32)
    queries = head_norm(projected[:, :inner_width], TOKENS)
    key_rows = head_norm(projected[:, inner_width:2 * inner_width], TOKENS)
    values = projected[:, 2 * inner_width:].astype(jnp.bfloat16).reshape(TOKENS, HEADS, HEAD)
    query_blocks = queries.reshape(N_SEQ, blocks, BLOCK, HEADS, HEAD)
    key_blocks = key_rows.reshape(N_SEQ, blocks, BLOCK, HEADS, HEAD)
    value_blocks = values.reshape(N_SEQ, blocks, BLOCK, HEADS, HEAD)
    devices = jnp.arange(N_SEQ, dtype=jnp.int32)
    partners = jnp.stack([jnp.bitwise_xor(devices, jnp.int32(1 << bit_level)) for bit_level in range(LEVELS)], axis=1)
    chosen = mirrored_lookup_tile.astype(jnp.int32)
    far_keys = key_blocks[partners, chosen]
    far_values = value_blocks[partners, chosen]
    attended = lax.map(attend_device, (query_blocks, key_blocks, value_blocks, far_keys, far_values))
    attended = attended.reshape(TOKENS, inner_width)
    return (widened + jnp.dot(attended, out_weights, preferred_element_type=jnp.float32)).astype(jnp.bfloat16)

def reference(resident_microbatches, arriving_microbatch, prenormal_scaling, attention_triple_matrix, exit_projection_matrix, mirrored_lookup_tile):
    starting_result = []
    for tier_ordinal in range(SECTIONS):
        starting_result.append(transform_through_tier(resident_microbatches[tier_ordinal], prenormal_scaling[tier_ordinal], attention_triple_matrix[tier_ordinal], exit_projection_matrix[tier_ordinal], mirrored_lookup_tile))
    second_in = [arriving_microbatch] + starting_result[:-1]
    second_out = []
    for tier_ordinal in range(SECTIONS):
        second_out.append(transform_through_tier(second_in[tier_ordinal], prenormal_scaling[tier_ordinal], attention_triple_matrix[tier_ordinal], exit_projection_matrix[tier_ordinal], mirrored_lookup_tile))
    return jnp.stack([jnp.stack(starting_result), jnp.stack(second_out)])
```

```python
import functools

import jax
import jax.numpy as jnp
from jax import lax
from jax.experimental import pallas as pl
from jax.experimental.pallas import tpu as pltpu
from jax.sharding import PartitionSpec as P

HEADS = 8
HEAD = 128
BLOCK = 64
LEVELS = 4
WIDE = 256

epsilon = 1e-06


def swapped(x, axis, mask):
    return lax.ppermute(x, axis, [(i, i ^ mask) for i in range(lax.axis_size(axis))])


def from_behind(block, axis, distance):
    devices = range(lax.axis_size(axis))
    route = [(i - distance, i) for i in devices if i - distance in devices]
    return lax.ppermute(block, axis, route)


def row_norm(rows, gain):
    widened = rows.astype(jnp.float32)
    mean_square = jnp.mean(widened * widened, axis=-1, keepdims=True)
    return (widened * lax.rsqrt(mean_square + epsilon) * gain).astype(jnp.bfloat16)


def head_norm(one_head):
    mean_square = jnp.mean(one_head * one_head, axis=-1, keepdims=True)
    return (one_head * lax.rsqrt(mean_square + epsilon)).astype(jnp.bfloat16)


def layer_kernel(pieces, offsets, own_ref, far_ref, gain_ref, exit_ref, *rest):
    shards = rest[:pieces]
    out_ref, triple, leave, normed, queries, keys, values, attended, load_sem, exit_sem = rest[pieces:]
    inner = HEADS * HEAD
    rows = own_ref.shape[0]
    far_rows = far_ref.shape[0]
    piece_rows = shards[0].shape[0]
    exit_copy = pltpu.make_async_copy(exit_ref, leave, exit_sem)
    for third in range(3):
        for i, shard in enumerate(shards):
            spot = pl.multiple_of(offsets[i], piece_rows)
            pltpu.make_async_copy(
                shard.at[:, pl.ds(third * inner, inner)],
                triple.at[third, pl.ds(spot, piece_rows), :],
                load_sem.at[third],
            ).start()
    exit_copy.start()

    def loaded(third):
        pltpu.make_async_copy(triple.at[third], triple.at[third], load_sem.at[third]).wait()

    gain = gain_ref[...]
    normed[:rows] = row_norm(own_ref[...], gain)
    normed[rows:] = row_norm(far_ref[...], gain)
    loaded(0)
    for start in range(0, inner, WIDE):
        projected = jnp.dot(
            normed[:rows], triple[0, :, start : start + WIDE], preferred_element_type=jnp.float32
        )
        for head in range(0, WIDE, HEAD):
            queries[:, start + head : start + head + HEAD] = head_norm(projected[:, head : head + HEAD])
    loaded(1)
    for start in range(0, inner, WIDE):
        projected = jnp.dot(
            normed[...], triple[1, :, start : start + WIDE], preferred_element_type=jnp.float32
        )
        for head in range(0, WIDE, HEAD):
            keys[:, start + head : start + head + HEAD] = head_norm(projected[:, head : head + HEAD])
    loaded(2)
    for start in range(0, inner, WIDE):
        values[:, start : start + WIDE] = jnp.dot(
            normed[...], triple[2, :, start : start + WIDE], preferred_element_type=jnp.float32
        ).astype(jnp.bfloat16)
    reader = lax.broadcasted_iota(jnp.int32, (rows, rows + far_rows), 0) // BLOCK
    column = lax.broadcasted_iota(jnp.int32, (rows, rows + far_rows), 1)
    read = jnp.logical_or(column >= rows, column // BLOCK == reader)
    score_scale = HEAD ** (-0.5)
    for start in range(0, inner, HEAD):
        span = slice(start, start + HEAD)
        scores = (
            lax.dot_general(
                queries[:, span],
                keys[:, span],
                (((1,), (1,)), ((), ())),
                preferred_element_type=jnp.float32,
            )
            * score_scale
        )
        exps = jnp.where(read, jnp.exp(scores), 0.0)
        weights = (exps / jnp.sum(exps, axis=-1, keepdims=True)).astype(jnp.bfloat16)
        attended[:, span] = jnp.dot(
            weights, values[:, span], preferred_element_type=jnp.float32
        ).astype(jnp.bfloat16)
    exit_copy.wait()
    for start in range(0, own_ref.shape[1], WIDE):
        span = slice(start, start + WIDE)
        out_ref[:, span] = (
            own_ref[:, span].astype(jnp.float32)
            + jnp.dot(attended[...], leave[:, span], preferred_element_type=jnp.float32)
        ).astype(jnp.bfloat16)


def layer(own, far, gain, exit_matrix, offsets, shards):
    rows, width = own.shape
    far_rows = far.shape[0]
    inner = HEADS * HEAD
    in_vmem = pl.BlockSpec(memory_space=pltpu.VMEM)
    anywhere = pl.BlockSpec(memory_space=pl.ANY)
    return pl.pallas_call(
        functools.partial(layer_kernel, len(shards)),
        out_shape=jax.ShapeDtypeStruct((rows, width), jnp.bfloat16),
        in_specs=[pl.BlockSpec(memory_space=pltpu.SMEM), in_vmem, in_vmem, in_vmem, anywhere]
        + [anywhere] * len(shards),
        out_specs=in_vmem,
        scratch_shapes=[
            pltpu.VMEM((3, width, inner), jnp.bfloat16),
            pltpu.VMEM((inner, width), jnp.bfloat16),
            pltpu.VMEM((rows + far_rows, width), jnp.bfloat16),
            pltpu.VMEM((rows, inner), jnp.bfloat16),
            pltpu.VMEM((rows + far_rows, inner), jnp.bfloat16),
            pltpu.VMEM((rows + far_rows, inner), jnp.bfloat16),
            pltpu.VMEM((rows, inner), jnp.bfloat16),
            pltpu.SemaphoreType.DMA((3,)),
            pltpu.SemaphoreType.DMA,
        ],
        compiler_params=pltpu.CompilerParams(vmem_limit_bytes=40 * 1024 * 1024),
        cost_estimate=pl.CostEstimate(flops=2_400_000_000, bytes_accessed=9_000_000, transcendentals=400_000),
    )(offsets, own, far, gain, exit_matrix, *shards)


def gathered(shard):
    devices = lax.axis_size("seq")
    me = lax.axis_index("seq")
    rows = shard.shape[0]
    if devices != 16:
        whole = lax.all_gather(shard, "seq", axis=0, tiled=True)
        return [whole], jnp.zeros((1,), jnp.int32)
    held = {0: shard}
    for mask in (4, 8, 12):
        held[mask] = swapped(shard, "seq", mask)
    for mask in (0, 4, 8, 12):
        held[mask | 2] = swapped(held[mask], "seq", 2)
    for mask in (0, 4, 2, 8, 6, 12, 10, 14):
        held[mask | 1] = swapped(held[mask], "seq", 1)
    order = sorted(held)
    offsets = jnp.stack([jnp.bitwise_xor(me, mask) * rows for mask in order]).astype(jnp.int32)
    return [held[mask] for mask in order], offsets


def partner_rows(own, lookup):
    me = lax.axis_index("seq")
    remote = []
    for level in range(LEVELS):
        partner = jnp.bitwise_xor(me, jnp.int32(1 << level))
        requested = lookup[partner, level]
        chosen = lax.dynamic_slice_in_dim(own, requested * BLOCK, BLOCK, 0)
        remote.append(swapped(chosen, "seq", 1 << level))
    return jnp.concatenate(remote, axis=0)


def per_device(resident, arriving, gain, triple, exit_matrix, lookup):
    section = lax.axis_index("section")
    shards, offsets = gathered(triple[0])
    first_in = resident[0]
    first_out = layer(first_in, partner_rows(first_in, lookup), gain, exit_matrix[0], offsets, shards)
    moved = from_behind(first_out, "section", 1)
    second_in = jnp.where(section == 0, arriving, moved)
    second_out = layer(second_in, partner_rows(second_in, lookup), gain, exit_matrix[0], offsets, shards)
    return jnp.stack([first_out, second_out])[:, None]


def solution(mesh):
    placed = (
        P("section", "seq", None),
        P("seq", None),
        P("section", None),
        P("section", "seq", None),
        P("section", None, None),
        P(),
    )
    return jax.shard_map(
        per_device,
        mesh=mesh,
        in_specs=placed,
        out_specs=P(None, "section", "seq", None),
        check_vma=False,
    )
```

```python
import functools

import jax
import jax.numpy as jnp
from jax import lax
from jax.experimental import pallas as pl
from jax.experimental.pallas import tpu as pltpu
from jax.sharding import PartitionSpec as P

HEADS = 8
HEAD = 128
BLOCK = 64
LEVELS = 4
WIDE = 256
MIB = 1024 * 1024

epsilon = 1e-06

in_vmem = pl.BlockSpec(memory_space=pltpu.VMEM)
in_smem = pl.BlockSpec(memory_space=pltpu.SMEM)
anywhere = pl.BlockSpec(memory_space=pl.ANY)


def swapped(x, axis, mask):
    return lax.ppermute(x, axis, [(i, i ^ mask) for i in range(lax.axis_size(axis))])


def from_behind(block, axis, distance):
    devices = range(lax.axis_size(axis))
    route = [(i - distance, i) for i in devices if i - distance in devices]
    return lax.ppermute(block, axis, route)


def after(x, *others):
    return lax.optimization_barrier((x, *others))[0]


def row_norm(rows, gain):
    widened = rows.astype(jnp.float32)
    mean_square = jnp.mean(widened * widened, axis=-1, keepdims=True)
    return (widened * lax.rsqrt(mean_square + epsilon) * gain).astype(jnp.bfloat16)


def head_norm(one_head):
    mean_square = jnp.mean(one_head * one_head, axis=-1, keepdims=True)
    return (one_head * lax.rsqrt(mean_square + epsilon)).astype(jnp.bfloat16)


def choose_kernel(wanted, moved_ref, arriving_ref, own_ref, *chosen):
    first = lax.axis_index("section") == 0

    @pl.when(first)
    def _():
        own_ref[...] = arriving_ref[...]

    @pl.when(jnp.logical_not(first))
    def _():
        own_ref[...] = moved_ref[...]

    shape = chosen[0].shape
    for level in range(LEVELS):
        asked = jnp.broadcast_to(wanted[level : level + 1, :1], shape)
        block = own_ref[:BLOCK].astype(jnp.float32)
        for i in range(1, own_ref.shape[0] // BLOCK):
            block = jnp.where(asked == i, own_ref[i * BLOCK : (i + 1) * BLOCK].astype(jnp.float32), block)
        chosen[level][...] = block.astype(own_ref.dtype)


def choose(wanted, moved, arriving):
    rows, width = moved.shape
    block = jax.ShapeDtypeStruct((BLOCK, width), moved.dtype)
    own, *chosen = pl.pallas_call(
        choose_kernel,
        out_shape=[jax.ShapeDtypeStruct((rows, width), moved.dtype)] + [block] * LEVELS,
        in_specs=[in_vmem] * 3,
        out_specs=[in_vmem] * (1 + LEVELS),
        compiler_params=pltpu.CompilerParams(vmem_limit_bytes=4 * MIB),
    )(wanted, moved, arriving)
    return own, chosen


def origin(behind, beside, twin):
    me = lax.axis_index("seq")
    plane = lax.rem(me // 4 + 4 - behind, 4)
    return plane * 4 + jnp.bitwise_xor(lax.rem(me, 4), 2 * beside + twin)


def assemble_kernel(places, *refs):
    pieces, (triple, sem) = refs[:-2], refs[-2:]
    rows, width = pieces[0].shape
    copies = []
    for i, (piece, hops) in enumerate(zip(pieces, places)):
        spot = pl.multiple_of(origin(*hops) * rows, rows)
        copies.append(pltpu.make_async_copy(piece, triple.at[pl.ds(spot, rows), :], sem.at[i]))
        copies[-1].start()
    spot = pl.multiple_of(origin(3, 1, 0) // 2 * (2 * rows), 2 * rows)
    triple[pl.ds(spot, 2 * rows), :] = jnp.zeros((2 * rows, width), triple.dtype)
    for copy in copies:
        copy.wait()


def assembled(pieces, places):
    rows, width = pieces[0].shape
    return pl.pallas_call(
        functools.partial(assemble_kernel, places),
        out_shape=pltpu.VMEM((rows * lax.axis_size("seq"), width), pieces[0].dtype),
        in_specs=[anywhere] * len(pieces),
        out_specs=in_vmem,
        scratch_shapes=[pltpu.SemaphoreType.DMA((len(pieces),))],
        compiler_params=pltpu.CompilerParams(vmem_limit_bytes=8 * MIB),
        cost_estimate=pl.CostEstimate(flops=0, bytes_accessed=12_000_000, transcendentals=0),
    )(*pieces)


def attend(own_ref, fars, gain_ref, triple, exit_ref, latest, put, normed, queries, keys, values, attended, last):
    inner = HEADS * HEAD
    rows = own_ref.shape[0]
    far_rows = LEVELS * BLOCK
    gain = gain_ref[...]
    normed[:rows] = row_norm(own_ref[...], gain)
    for level in range(LEVELS):
        normed[rows + level * BLOCK : rows + (level + 1) * BLOCK] = row_norm(fars[level][...], gain)
    if latest:
        part = latest[0].shape[0]
        core = lax.rem(lax.axis_index("seq"), 2)
        last[pl.ds(pl.multiple_of(core * part, part), part), :] = latest[0][...]
        last[pl.ds(pl.multiple_of((1 - core) * part, part), part), :] = latest[1][...]
        spot = pl.multiple_of(origin(3, 1, 0) // 2 * (2 * part), 2 * part)
        late_columns = normed[:, pl.ds(spot, 2 * part)]

    def projection(count, start):
        span = slice(start, start + WIDE)
        result = jnp.dot(normed[:count], triple[:, span], preferred_element_type=jnp.float32)
        if latest:
            result += jnp.dot(late_columns[:count], last[:, span], preferred_element_type=jnp.float32)
        return result

    for start in range(0, inner, WIDE):
        projected = projection(rows, start)
        for head in range(0, WIDE, HEAD):
            queries[:, start + head : start + head + HEAD] = head_norm(projected[:, head : head + HEAD])
    for start in range(0, inner, WIDE):
        projected = projection(rows + far_rows, inner + start)
        for head in range(0, WIDE, HEAD):
            keys[:, start + head : start + head + HEAD] = head_norm(projected[:, head : head + HEAD])
    for start in range(0, inner, WIDE):
        values[:, start : start + WIDE] = projection(rows + far_rows, 2 * inner + start).astype(jnp.bfloat16)
    reader = lax.broadcasted_iota(jnp.int32, (rows, rows + far_rows), 0) // BLOCK
    column = lax.broadcasted_iota(jnp.int32, (rows, rows + far_rows), 1)
    read = jnp.logical_or(column >= rows, column // BLOCK == reader)
    score_scale = HEAD ** (-0.5)
    for start in range(0, inner, HEAD):
        span = slice(start, start + HEAD)
        scores = (
            lax.dot_general(
                queries[:, span],
                keys[:, span],
                (((1,), (1,)), ((), ())),
                preferred_element_type=jnp.float32,
            )
            * score_scale
        )
        exps = jnp.where(read, jnp.exp(scores), 0.0)
        weights = (exps / jnp.sum(exps, axis=-1, keepdims=True)).astype(jnp.bfloat16)
        attended[:, span] = jnp.dot(weights, values[:, span], preferred_element_type=jnp.float32).astype(jnp.bfloat16)
    for start in range(0, own_ref.shape[1], WIDE):
        span = slice(start, start + WIDE)
        put[:, span] = (
            own_ref[:, span].astype(jnp.float32)
            + jnp.dot(attended[...], exit_ref[:, span], preferred_element_type=jnp.float32)
        ).astype(jnp.bfloat16)


def first_kernel(late, triple, own_ref, *refs):
    fars, refs = refs[:LEVELS], refs[LEVELS:]
    gain_ref, exit_ref, *refs = refs
    latest, refs = refs[:late], refs[late:]
    out_ref, *scratch = refs
    attend(own_ref, fars, gain_ref, triple, exit_ref, latest, out_ref, *scratch)


def second_kernel(late, triple, own_ref, *refs):
    fars, refs = refs[:LEVELS], refs[LEVELS:]
    gain_ref, exit_ref, *refs = refs
    latest, refs = refs[:late], refs[late:]
    first_ref, out_ref, result, sems, *scratch = refs
    early = pltpu.make_async_copy(first_ref, out_ref.at[0], sems.at[0])
    early.start()
    attend(own_ref, fars, gain_ref, triple, exit_ref, latest, result, *scratch)
    finish = pltpu.make_async_copy(result, out_ref.at[1], sems.at[1])
    finish.start()
    early.wait()
    finish.wait()


def scratch_of(rows, width, triple, latest):
    inner = HEADS * HEAD
    reach = rows + LEVELS * BLOCK
    late_rows = 2 * latest[0].shape[0] if latest else 16
    return [
        pltpu.VMEM((reach, width), jnp.bfloat16),
        pltpu.VMEM((rows, inner), jnp.bfloat16),
        pltpu.VMEM((reach, inner), jnp.bfloat16),
        pltpu.VMEM((reach, inner), jnp.bfloat16),
        pltpu.VMEM((rows, inner), jnp.bfloat16),
        pltpu.VMEM((late_rows, triple.shape[1]), jnp.bfloat16),
    ]


cost = pl.CostEstimate(flops=2_400_000_000, bytes_accessed=9_000_000, transcendentals=400_000)


def first_layer(triple, own, fars, gain, exit_matrix, latest):
    return pl.pallas_call(
        functools.partial(first_kernel, len(latest)),
        out_shape=jax.ShapeDtypeStruct(own.shape, own.dtype),
        in_specs=[in_vmem] * (4 + LEVELS + len(latest)),
        out_specs=in_vmem,
        scratch_shapes=scratch_of(*own.shape, triple, latest),
        compiler_params=pltpu.CompilerParams(vmem_limit_bytes=16 * MIB),
        cost_estimate=cost,
    )(triple, own, *fars, gain, exit_matrix, *latest)


def second_layer(triple, own, fars, gain, exit_matrix, latest, first_out):
    return pl.pallas_call(
        functools.partial(second_kernel, len(latest)),
        out_shape=jax.ShapeDtypeStruct((2,) + own.shape, own.dtype),
        in_specs=[in_vmem] * (5 + LEVELS + len(latest)),
        out_specs=anywhere,
        scratch_shapes=[pltpu.VMEM(own.shape, own.dtype), pltpu.SemaphoreType.DMA((2,))]
        + scratch_of(*own.shape, triple, latest),
        compiler_params=pltpu.CompilerParams(vmem_limit_bytes=16 * MIB),
        cost_estimate=cost,
    )(triple, own, *fars, gain, exit_matrix, *latest, first_out)


def gathered(shard, chosen):
    def around(x):
        return lax.ppermute(x, "seq", [(i, (i + 4) % 16) for i in range(16)])

    def beside(x):
        return swapped(x, "seq", 2)

    def twin(x):
        return swapped(x, "seq", 1)

    r1 = around(shard)
    x0 = beside(shard)
    c0 = twin(shard)
    r2 = around(r1)
    near = [twin(chosen[0]), beside(chosen[1])]
    x1 = beside(after(r1, near[1]))
    cr1 = twin(after(r1, near[0]))
    cx0 = twin(x0)
    r3 = around(after(r2, c0, cr1, cx0))
    x2 = beside(after(r2, c0))
    x3 = beside(r3)
    far = [swapped(after(chosen[level], r3), "seq", 1 << level) for level in (3, 2)]
    cr2 = twin(r2)
    cx1 = twin(x1)
    cr3 = twin(r3)
    cx2 = twin(x2)
    early = [
        (shard, 0, 0, 0),
        (c0, 0, 0, 1),
        (x0, 0, 1, 0),
        (cx0, 0, 1, 1),
        (r1, 1, 0, 0),
        (cr1, 1, 0, 1),
        (x1, 1, 1, 0),
        (cx1, 1, 1, 1),
        (r2, 2, 0, 0),
        (cr2, 2, 0, 1),
        (x2, 2, 1, 0),
        (cx2, 2, 1, 1),
        (r3, 3, 0, 0),
        (cr3, 3, 0, 1),
    ]
    triple = assembled([piece for piece, *_ in early], [tuple(hops) for _, *hops in early])
    return triple, [x3, twin(after(x3, triple, *far))], near + far[::-1]


def partner_rows(chosen):
    far = [swapped(chosen[level], "seq", 1 << level) for level in range(LEVELS - 1, -1, -1)]
    return far[::-1]


def per_device(resident, arriving, gain, triple, exit_matrix, lookup):
    first_in = resident[0]
    me = lax.axis_index("seq")
    levels = jnp.arange(8, dtype=jnp.int32)
    partner = jnp.bitwise_xor(me, jnp.left_shift(1, levels % LEVELS))
    wanted = jnp.broadcast_to(lookup[partner, levels % LEVELS][:, None], (8, 128))
    _, chosen = choose(wanted, first_in, first_in)
    if lax.axis_size("seq") == 16:
        triple, latest, fars = gathered(triple[0], chosen)
    else:
        triple = lax.all_gather(triple[0], "seq", axis=0, tiled=True)
        latest = []
        fars = partner_rows(chosen)
    first_out = first_layer(triple, first_in, fars, gain, exit_matrix[0], latest)
    moved = from_behind(first_out, "section", 1)
    second_in, chosen = choose(wanted, moved, arriving)
    fars = partner_rows(chosen)
    return second_layer(triple, second_in, fars, gain, exit_matrix[0], latest, first_out)[:, None]


def solution(mesh):
    placed = (
        P("section", "seq", None),
        P("seq", None),
        P("section", None),
        P("section", "seq", None),
        P("section", None, None),
        P(),
    )
    return jax.shard_map(
        per_device,
        mesh=mesh,
        in_specs=placed,
        out_specs=P(None, "section", "seq", None),
        check_vma=False,
    )
```

```python
import functools
import math

import jax
import jax.numpy as jnp
from jax import lax
from jax.experimental import pallas as pl
from jax.experimental.pallas import tpu as pltpu
from jax.sharding import PartitionSpec as P

HEADS = 8
HEAD = 128
BLOCK = 64
LEVELS = 4
WIDE = 256
MIB = 1024 * 1024

epsilon = 1e-06

in_vmem = pl.BlockSpec(memory_space=pltpu.VMEM)
in_smem = pl.BlockSpec(memory_space=pltpu.SMEM)
anywhere = pl.BlockSpec(memory_space=pl.ANY)


def swapped(x, axis, mask):
    return lax.ppermute(x, axis, [(i, i ^ mask) for i in range(lax.axis_size(axis))])


def from_behind(block, axis, distance):
    devices = range(lax.axis_size(axis))
    route = [(i - distance, i) for i in devices if i - distance in devices]
    return lax.ppermute(block, axis, route)


def after(x, *others):
    return lax.optimization_barrier((x, *others))[0]


def row_norm(rows, gain):
    widened = rows.astype(jnp.float32)
    mean_square = jnp.mean(widened * widened, axis=-1, keepdims=True)
    return (widened * lax.rsqrt(mean_square + epsilon) * gain).astype(jnp.bfloat16)


def head_norm(one_head):
    mean_square = jnp.mean(one_head * one_head, axis=-1, keepdims=True)
    return (one_head * lax.rsqrt(mean_square + epsilon)).astype(jnp.bfloat16)


def choose_kernel(wanted, moved_ref, arriving_ref, own_ref, *chosen):
    first = lax.axis_index("section") == 0

    @pl.when(first)
    def _():
        own_ref[...] = arriving_ref[...]

    @pl.when(jnp.logical_not(first))
    def _():
        own_ref[...] = moved_ref[...]

    shape = chosen[0].shape
    for level in range(LEVELS):
        asked = jnp.broadcast_to(wanted[level : level + 1, :1], shape)
        block = own_ref[:BLOCK].astype(jnp.float32)
        for i in range(1, own_ref.shape[0] // BLOCK):
            block = jnp.where(asked == i, own_ref[i * BLOCK : (i + 1) * BLOCK].astype(jnp.float32), block)
        chosen[level][...] = block.astype(own_ref.dtype)


def choose(wanted, moved, arriving):
    rows, width = moved.shape
    block = jax.ShapeDtypeStruct((BLOCK, width), moved.dtype)
    own, *chosen = pl.pallas_call(
        choose_kernel,
        out_shape=[jax.ShapeDtypeStruct((rows, width), moved.dtype)] + [block] * LEVELS,
        in_specs=[in_vmem] * 3,
        out_specs=[in_vmem] * (1 + LEVELS),
        compiler_params=pltpu.CompilerParams(vmem_limit_bytes=4 * MIB),
    )(wanted, moved, arriving)
    return own, chosen


def origin(behind, beside, twin):
    me = lax.axis_index("seq")
    plane = me // 4
    spot = jnp.bitwise_and(jnp.bitwise_xor(plane, plane // 2) + 4 - behind, 3)
    plane = jnp.bitwise_xor(spot, spot // 2)
    return plane * 4 + jnp.bitwise_xor(lax.rem(me, 4), 2 * beside + twin)


def assemble_kernel(places, *refs):
    pieces, (triple, sem) = refs[:-2], refs[-2:]
    rows, width = pieces[0].shape
    copies = []
    for i, (piece, hops) in enumerate(zip(pieces, places)):
        spot = pl.multiple_of(origin(*hops) * rows, rows)
        copies.append(pltpu.make_async_copy(piece, triple.at[pl.ds(spot, rows), :], sem.at[i]))
        copies[-1].start()
    spot = pl.multiple_of(origin(3, 1, 0) // 2 * (2 * rows), 2 * rows)
    triple[pl.ds(spot, 2 * rows), :] = jnp.zeros((2 * rows, width), triple.dtype)
    for copy in copies:
        copy.wait()


def assembled(pieces, places):
    rows, width = pieces[0].shape
    return pl.pallas_call(
        functools.partial(assemble_kernel, places),
        out_shape=pltpu.VMEM((rows * lax.axis_size("seq"), width), pieces[0].dtype),
        in_specs=[anywhere] * len(pieces),
        out_specs=in_vmem,
        scratch_shapes=[pltpu.SemaphoreType.DMA((len(pieces),))],
        compiler_params=pltpu.CompilerParams(vmem_limit_bytes=8 * MIB),
        cost_estimate=pl.CostEstimate(flops=0, bytes_accessed=12_000_000, transcendentals=0),
    )(*pieces)


def attend(own_ref, fars, gain_ref, triple, exit_ref, latest, put, normed, queries, keys, values, attended, last):
    inner = HEADS * HEAD
    rows = own_ref.shape[0]
    far_rows = LEVELS * BLOCK
    gain = gain_ref[...]
    normed[:rows] = row_norm(own_ref[...], gain)
    for level in range(LEVELS):
        normed[rows + level * BLOCK : rows + (level + 1) * BLOCK] = row_norm(fars[level][...], gain)
    if latest:
        part = latest[0].shape[0]
        core = lax.rem(lax.axis_index("seq"), 2)
        last[pl.ds(pl.multiple_of(core * part, part), part), :] = latest[0][...]
        last[pl.ds(pl.multiple_of((1 - core) * part, part), part), :] = latest[1][...]
        spot = pl.multiple_of(origin(3, 1, 0) // 2 * (2 * part), 2 * part)
        late_columns = normed[:, pl.ds(spot, 2 * part)]

    def projection(count, start):
        span = slice(start, start + WIDE)
        result = jnp.dot(normed[:count], triple[:, span], preferred_element_type=jnp.float32)
        if latest:
            result += jnp.dot(late_columns[:count], last[:, span], preferred_element_type=jnp.float32)
        return result

    for start in range(0, inner, WIDE):
        projected = projection(rows, start)
        for head in range(0, WIDE, HEAD):
            queries[:, start + head : start + head + HEAD] = head_norm(projected[:, head : head + HEAD])
    for start in range(0, inner, WIDE):
        projected = projection(rows + far_rows, inner + start)
        for head in range(0, WIDE, HEAD):
            keys[:, start + head : start + head + HEAD] = head_norm(projected[:, head : head + HEAD])
    for start in range(0, inner, WIDE):
        values[:, start : start + WIDE] = projection(rows + far_rows, 2 * inner + start).astype(jnp.bfloat16)
    reader = lax.broadcasted_iota(jnp.int32, (rows, rows), 0) // BLOCK
    column = lax.broadcasted_iota(jnp.int32, (rows, rows), 1) // BLOCK
    read = reader == column
    score_scale = HEAD ** (-0.5) * math.log2(math.e)
    spans = [slice(start, start + HEAD) for start in range(0, inner, HEAD)]
    scores = [
        lax.dot_general(
            queries[:, span], keys[:, span], (((1,), (1,)), ((), ())), preferred_element_type=jnp.float32
        )
        for span in spans
    ]
    weights = []
    for score in scores:
        exps = jnp.exp2(score * score_scale)
        exps = jnp.concatenate([jnp.where(read, exps[:, :rows], 0.0), exps[:, rows:]], axis=1)
        total = jnp.sum(exps, axis=-1, keepdims=True)
        weights.append((exps * (1.0 / total)).astype(jnp.bfloat16))
    for span, weight in zip(spans, weights):
        attended[:, span] = jnp.dot(weight, values[:, span], preferred_element_type=jnp.float32).astype(jnp.bfloat16)
    for start in range(0, own_ref.shape[1], WIDE):
        span = slice(start, start + WIDE)
        put[:, span] = (
            own_ref[:, span].astype(jnp.float32)
            + jnp.dot(attended[...], exit_ref[:, span], preferred_element_type=jnp.float32)
        ).astype(jnp.bfloat16)


def first_kernel(late, triple, own_ref, *refs):
    fars, refs = refs[:LEVELS], refs[LEVELS:]
    gain_ref, exit_ref, *refs = refs
    latest, refs = refs[:late], refs[late:]
    out_ref, *scratch = refs
    attend(own_ref, fars, gain_ref, triple, exit_ref, latest, out_ref, *scratch)


def second_kernel(late, triple, own_ref, *refs):
    fars, refs = refs[:LEVELS], refs[LEVELS:]
    gain_ref, exit_ref, *refs = refs
    latest, refs = refs[:late], refs[late:]
    first_ref, out_ref, result, sems, *scratch = refs
    early = pltpu.make_async_copy(first_ref, out_ref.at[0], sems.at[0])
    early.start()
    attend(own_ref, fars, gain_ref, triple, exit_ref, latest, result, *scratch)
    finish = pltpu.make_async_copy(result, out_ref.at[1], sems.at[1])
    finish.start()
    early.wait()
    finish.wait()


def scratch_of(rows, width, triple, latest):
    inner = HEADS * HEAD
    reach = rows + LEVELS * BLOCK
    late_rows = 2 * latest[0].shape[0] if latest else 16
    return [
        pltpu.VMEM((reach, width), jnp.bfloat16),
        pltpu.VMEM((rows, inner), jnp.bfloat16),
        pltpu.VMEM((reach, inner), jnp.bfloat16),
        pltpu.VMEM((reach, inner), jnp.bfloat16),
        pltpu.VMEM((rows, inner), jnp.bfloat16),
        pltpu.VMEM((late_rows, triple.shape[1]), jnp.bfloat16),
    ]


cost = pl.CostEstimate(flops=2_400_000_000, bytes_accessed=9_000_000, transcendentals=400_000)


def first_layer(triple, own, fars, gain, exit_matrix, latest):
    return pl.pallas_call(
        functools.partial(first_kernel, len(latest)),
        out_shape=jax.ShapeDtypeStruct(own.shape, own.dtype),
        in_specs=[in_vmem] * (4 + LEVELS + len(latest)),
        out_specs=in_vmem,
        scratch_shapes=scratch_of(*own.shape, triple, latest),
        compiler_params=pltpu.CompilerParams(vmem_limit_bytes=16 * MIB),
        cost_estimate=cost,
    )(triple, own, *fars, gain, exit_matrix, *latest)


def second_layer(triple, own, fars, gain, exit_matrix, latest, first_out):
    return pl.pallas_call(
        functools.partial(second_kernel, len(latest)),
        out_shape=jax.ShapeDtypeStruct((2,) + own.shape, own.dtype),
        in_specs=[in_vmem] * (5 + LEVELS + len(latest)),
        out_specs=anywhere,
        scratch_shapes=[pltpu.VMEM(own.shape, own.dtype), pltpu.SemaphoreType.DMA((2,))]
        + scratch_of(*own.shape, triple, latest),
        compiler_params=pltpu.CompilerParams(vmem_limit_bytes=16 * MIB),
        cost_estimate=cost,
    )(triple, own, *fars, gain, exit_matrix, *latest, first_out)


def gathered(shard, chosen):
    ring = [0, 1, 3, 2]
    onward = {ring[i]: ring[(i + 1) % 4] for i in range(4)}

    def around(x):
        return lax.ppermute(x, "seq", [(i, onward[i // 4] * 4 + i % 4) for i in range(16)])

    def back(x):
        return lax.ppermute(x, "seq", [(onward[i // 4] * 4 + i % 4, i) for i in range(16)])

    def beside(x):
        return swapped(x, "seq", 2)

    def twin(x):
        return swapped(x, "seq", 1)

    r1 = around(shard)
    x0 = beside(shard)
    c0 = twin(shard)
    near = [twin(chosen[0]), beside(after(chosen[1], c0))]
    r2 = around(r1)
    cr1 = twin(r1)
    x1 = beside(after(r1, near[1]))
    l1 = back(after(shard, cr1))
    cx0 = twin(x0)
    x2 = beside(after(r2, cx0, cr1))
    cr2 = twin(r2)
    cx1 = twin(x1)
    x3 = beside(after(l1, cx1, cr2))
    far = [swapped(after(chosen[level], l1), "seq", 1 << level) for level in (3, 2)]
    cl1 = twin(l1)
    cx2 = twin(x2)
    early = [
        (shard, 0, 0, 0),
        (c0, 0, 0, 1),
        (r1, 1, 0, 0),
        (cr1, 1, 0, 1),
        (l1, 3, 0, 0),
        (cl1, 3, 0, 1),
        (r2, 2, 0, 0),
        (cr2, 2, 0, 1),
        (x0, 0, 1, 0),
        (cx0, 0, 1, 1),
        (x1, 1, 1, 0),
        (cx1, 1, 1, 1),
        (x2, 2, 1, 0),
        (cx2, 2, 1, 1),
    ]
    triple = assembled([piece for piece, *_ in early], [tuple(hops) for _, *hops in early])
    return triple, [x3, twin(after(x3, triple, *far))], near + far[::-1]


def partner_rows(chosen):
    twin = swapped(chosen[0], "seq", 1)
    late = [after(block, twin) for block in chosen[1:-1]] + [chosen[-1]]
    return [twin] + [swapped(block, "seq", 2 << level) for level, block in enumerate(late)]


def per_device(resident, arriving, gain, triple, exit_matrix, lookup):
    first_in = resident[0]
    me = lax.axis_index("seq")
    levels = jnp.arange(8, dtype=jnp.int32)
    partner = jnp.bitwise_xor(me, jnp.left_shift(1, levels % LEVELS))
    wanted = jnp.broadcast_to(lookup[partner, levels % LEVELS][:, None], (8, 128))
    _, chosen = choose(wanted, first_in, first_in)
    if lax.axis_size("seq") == 16:
        triple, latest, fars = gathered(triple[0], chosen)
    else:
        triple = lax.all_gather(triple[0], "seq", axis=0, tiled=True)
        latest = []
        fars = partner_rows(chosen)
    first_out = first_layer(triple, first_in, fars, gain, exit_matrix[0], latest)
    moved = from_behind(first_out, "section", 1)
    second_in, chosen = choose(wanted, moved, arriving)
    fars = partner_rows(chosen)
    return second_layer(triple, second_in, fars, gain, exit_matrix[0], latest, first_out)[:, None]


def solution(mesh):
    placed = (
        P("section", "seq", None),
        P("seq", None),
        P("section", None),
        P("section", "seq", None),
        P("section", None, None),
        P(),
    )
    return jax.shard_map(
        per_device,
        mesh=mesh,
        in_specs=placed,
        out_specs=P(None, "section", "seq", None),
        check_vma=False,
    )
```

```python
import functools
import math

import jax
import jax.numpy as jnp
from jax import lax
from jax.experimental import pallas as pl
from jax.experimental.pallas import tpu as pltpu
from jax.sharding import PartitionSpec as P

HEADS = 8
HEAD = 128
BLOCK = 64
LEVELS = 4
WIDE = 256
MIB = 1024 * 1024

epsilon = 1e-06

in_vmem = pl.BlockSpec(memory_space=pltpu.VMEM)
in_smem = pl.BlockSpec(memory_space=pltpu.SMEM)
anywhere = pl.BlockSpec(memory_space=pl.ANY)


def swapped(x, axis, mask):
    return lax.ppermute(x, axis, [(i, i ^ mask) for i in range(lax.axis_size(axis))])


def from_behind(block, axis, distance):
    devices = range(lax.axis_size(axis))
    route = [(i - distance, i) for i in devices if i - distance in devices]
    return lax.ppermute(block, axis, route)


def after(x, *others):
    return lax.optimization_barrier((x, *others))[0]


def row_norm(rows, gain):
    widened = rows.astype(jnp.float32)
    mean_square = jnp.mean(widened * widened, axis=-1, keepdims=True)
    return (widened * lax.rsqrt(mean_square + epsilon) * gain).astype(jnp.bfloat16)


def head_norm(one_head):
    mean_square = jnp.mean(one_head * one_head, axis=-1, keepdims=True)
    return (one_head * lax.rsqrt(mean_square + epsilon)).astype(jnp.bfloat16)


def choose_kernel(wanted, moved_ref, arriving_ref, own_ref, *chosen):
    first = lax.axis_index("section") == 0

    @pl.when(first)
    def _():
        own_ref[...] = arriving_ref[...]

    @pl.when(jnp.logical_not(first))
    def _():
        own_ref[...] = moved_ref[...]

    shape = chosen[0].shape
    for level in range(LEVELS):
        asked = jnp.broadcast_to(wanted[level : level + 1, :1], shape)
        block = own_ref[:BLOCK].astype(jnp.float32)
        for i in range(1, own_ref.shape[0] // BLOCK):
            block = jnp.where(asked == i, own_ref[i * BLOCK : (i + 1) * BLOCK].astype(jnp.float32), block)
        chosen[level][...] = block.astype(own_ref.dtype)


def choose(wanted, moved, arriving):
    rows, width = moved.shape
    block = jax.ShapeDtypeStruct((BLOCK, width), moved.dtype)
    own, *chosen = pl.pallas_call(
        choose_kernel,
        out_shape=[jax.ShapeDtypeStruct((rows, width), moved.dtype)] + [block] * LEVELS,
        in_specs=[in_vmem] * 3,
        out_specs=[in_vmem] * (1 + LEVELS),
        compiler_params=pltpu.CompilerParams(vmem_limit_bytes=4 * MIB),
    )(wanted, moved, arriving)
    return own, chosen


def origin(behind, beside, twin):
    me = lax.axis_index("seq")
    plane = me // 4
    spot = jnp.bitwise_and(jnp.bitwise_xor(plane, plane // 2) + 4 - behind, 3)
    plane = jnp.bitwise_xor(spot, spot // 2)
    return plane * 4 + jnp.bitwise_xor(lax.rem(me, 4), 2 * beside + twin)


def assemble_kernel(places, *refs):
    pieces, (triple, sem) = refs[:-2], refs[-2:]
    rows, width = pieces[0].shape
    copies = []
    for i, (piece, hops) in enumerate(zip(pieces, places)):
        spot = pl.multiple_of(origin(*hops) * rows, rows)
        copies.append(pltpu.make_async_copy(piece, triple.at[pl.ds(spot, rows), :], sem.at[i]))
        copies[-1].start()
    spot = pl.multiple_of(origin(3, 1, 0) // 2 * (2 * rows), 2 * rows)
    triple[pl.ds(spot, 2 * rows), :] = jnp.zeros((2 * rows, width), triple.dtype)
    for copy in copies:
        copy.wait()


def assembled(pieces, places):
    rows, width = pieces[0].shape
    return pl.pallas_call(
        functools.partial(assemble_kernel, places),
        out_shape=pltpu.VMEM((rows * lax.axis_size("seq"), width), pieces[0].dtype),
        in_specs=[anywhere] * len(pieces),
        out_specs=in_vmem,
        scratch_shapes=[pltpu.SemaphoreType.DMA((len(pieces),))],
        compiler_params=pltpu.CompilerParams(vmem_limit_bytes=8 * MIB),
        cost_estimate=pl.CostEstimate(flops=0, bytes_accessed=12_000_000, transcendentals=0),
    )(*pieces)


def ahead_kernel(triple, own_ref, gain_ref, out_ref, normed):
    normed[...] = row_norm(own_ref[...], gain_ref[...])
    for start in range(0, triple.shape[1], WIDE):
        span = slice(start, start + WIDE)
        out_ref[:, span] = jnp.dot(normed[...], triple[:, span], preferred_element_type=jnp.float32)


def ahead(triple, own, gain):
    rows, width = own.shape
    return pl.pallas_call(
        ahead_kernel,
        out_shape=pltpu.VMEM((rows, triple.shape[1]), jnp.float32),
        in_specs=[in_vmem] * 3,
        out_specs=in_vmem,
        scratch_shapes=[pltpu.VMEM((rows, width), jnp.bfloat16)],
        compiler_params=pltpu.CompilerParams(vmem_limit_bytes=4 * MIB),
        cost_estimate=pl.CostEstimate(flops=800_000_000, bytes_accessed=8_000_000, transcendentals=0),
    )(triple, own, gain)


def attend(own_ref, started, fars, gain_ref, triple, exit_ref, latest, put, normed, queries, keys, values, attended, last):
    inner = HEADS * HEAD
    rows = own_ref.shape[0]
    far_rows = LEVELS * BLOCK
    gain = gain_ref[...]
    normed[:rows] = row_norm(own_ref[...], gain)
    for level in range(LEVELS):
        normed[rows + level * BLOCK : rows + (level + 1) * BLOCK] = row_norm(fars[level][...], gain)
    if latest:
        part = latest[0].shape[0]
        core = lax.rem(lax.axis_index("seq"), 2)
        last[pl.ds(pl.multiple_of(core * part, part), part), :] = latest[0][...]
        last[pl.ds(pl.multiple_of((1 - core) * part, part), part), :] = latest[1][...]
        spot = pl.multiple_of(origin(3, 1, 0) // 2 * (2 * part), 2 * part)
        late_columns = normed[:, pl.ds(spot, 2 * part)]

    def own_part(start):
        span = slice(start, start + WIDE)
        result = started[:, span]
        if latest:
            result += jnp.dot(late_columns[:rows], last[:, span], preferred_element_type=jnp.float32)
        return result

    def far_part(start):
        span = slice(start, start + WIDE)
        result = jnp.dot(normed[rows:], triple[:, span], preferred_element_type=jnp.float32)
        if latest:
            result += jnp.dot(late_columns[rows:], last[:, span], preferred_element_type=jnp.float32)
        return result

    for start in range(0, inner, WIDE):
        projected = own_part(start)
        for head in range(0, WIDE, HEAD):
            queries[:, start + head : start + head + HEAD] = head_norm(projected[:, head : head + HEAD])
    for start in range(0, inner, WIDE):
        near, far = own_part(inner + start), far_part(inner + start)
        for head in range(0, WIDE, HEAD):
            span = slice(start + head, start + head + HEAD)
            keys[:rows, span] = head_norm(near[:, head : head + HEAD])
            keys[rows:, span] = head_norm(far[:, head : head + HEAD])
    for start in range(0, inner, WIDE):
        span = slice(start, start + WIDE)
        values[:rows, span] = own_part(2 * inner + start).astype(jnp.bfloat16)
        values[rows:, span] = far_part(2 * inner + start).astype(jnp.bfloat16)
    reader = lax.broadcasted_iota(jnp.int32, (rows, rows), 0) // BLOCK
    column = lax.broadcasted_iota(jnp.int32, (rows, rows), 1) // BLOCK
    read = reader == column
    score_scale = HEAD ** (-0.5) * math.log2(math.e)
    spans = [slice(start, start + HEAD) for start in range(0, inner, HEAD)]
    scores = [
        lax.dot_general(
            queries[:, span], keys[:, span], (((1,), (1,)), ((), ())), preferred_element_type=jnp.float32
        )
        for span in spans
    ]
    weights = []
    for score in scores:
        exps = jnp.exp2(score * score_scale)
        exps = jnp.concatenate([jnp.where(read, exps[:, :rows], 0.0), exps[:, rows:]], axis=1)
        total = jnp.sum(exps, axis=-1, keepdims=True)
        weights.append((exps * (1.0 / total)).astype(jnp.bfloat16))
    for span, weight in zip(spans, weights):
        attended[:, span] = jnp.dot(weight, values[:, span], preferred_element_type=jnp.float32).astype(jnp.bfloat16)
    for start in range(0, own_ref.shape[1], WIDE):
        span = slice(start, start + WIDE)
        put[:, span] = (
            own_ref[:, span].astype(jnp.float32)
            + jnp.dot(attended[...], exit_ref[:, span], preferred_element_type=jnp.float32)
        ).astype(jnp.bfloat16)


def first_kernel(late, triple, own_ref, started, *refs):
    fars, refs = refs[:LEVELS], refs[LEVELS:]
    gain_ref, exit_ref, *refs = refs
    latest, refs = refs[:late], refs[late:]
    out_ref, *scratch = refs
    attend(own_ref, started, fars, gain_ref, triple, exit_ref, latest, out_ref, *scratch)


def second_kernel(late, triple, own_ref, started, *refs):
    fars, refs = refs[:LEVELS], refs[LEVELS:]
    gain_ref, exit_ref, *refs = refs
    latest, refs = refs[:late], refs[late:]
    first_ref, out_ref, result, sems, *scratch = refs
    early = pltpu.make_async_copy(first_ref, out_ref.at[0], sems.at[0])
    early.start()
    attend(own_ref, started, fars, gain_ref, triple, exit_ref, latest, result, *scratch)
    finish = pltpu.make_async_copy(result, out_ref.at[1], sems.at[1])
    finish.start()
    early.wait()
    finish.wait()


def scratch_of(rows, width, triple, latest):
    inner = HEADS * HEAD
    reach = rows + LEVELS * BLOCK
    late_rows = 2 * latest[0].shape[0] if latest else 16
    return [
        pltpu.VMEM((reach, width), jnp.bfloat16),
        pltpu.VMEM((rows, inner), jnp.bfloat16),
        pltpu.VMEM((reach, inner), jnp.bfloat16),
        pltpu.VMEM((reach, inner), jnp.bfloat16),
        pltpu.VMEM((rows, inner), jnp.bfloat16),
        pltpu.VMEM((late_rows, triple.shape[1]), jnp.bfloat16),
    ]


cost = pl.CostEstimate(flops=2_400_000_000, bytes_accessed=9_000_000, transcendentals=400_000)


def first_layer(triple, own, started, fars, gain, exit_matrix, latest):
    return pl.pallas_call(
        functools.partial(first_kernel, len(latest)),
        out_shape=jax.ShapeDtypeStruct(own.shape, own.dtype),
        in_specs=[in_vmem] * (5 + LEVELS + len(latest)),
        out_specs=in_vmem,
        scratch_shapes=scratch_of(*own.shape, triple, latest),
        compiler_params=pltpu.CompilerParams(vmem_limit_bytes=16 * MIB),
        cost_estimate=cost,
    )(triple, own, started, *fars, gain, exit_matrix, *latest)


def second_layer(triple, own, started, fars, gain, exit_matrix, latest, first_out):
    return pl.pallas_call(
        functools.partial(second_kernel, len(latest)),
        out_shape=jax.ShapeDtypeStruct((2,) + own.shape, own.dtype),
        in_specs=[in_vmem] * (6 + LEVELS + len(latest)),
        out_specs=anywhere,
        scratch_shapes=[pltpu.VMEM(own.shape, own.dtype), pltpu.SemaphoreType.DMA((2,))]
        + scratch_of(*own.shape, triple, latest),
        compiler_params=pltpu.CompilerParams(vmem_limit_bytes=16 * MIB),
        cost_estimate=cost,
    )(triple, own, started, *fars, gain, exit_matrix, *latest, first_out)


def gathered(shard, chosen, own, gain):
    ring = [0, 1, 3, 2]
    onward = {ring[i]: ring[(i + 1) % 4] for i in range(4)}

    def around(x):
        return lax.ppermute(x, "seq", [(i, onward[i // 4] * 4 + i % 4) for i in range(16)])

    def back(x):
        return lax.ppermute(x, "seq", [(onward[i // 4] * 4 + i % 4, i) for i in range(16)])

    def beside(x):
        return swapped(x, "seq", 2)

    def twin(x):
        return swapped(x, "seq", 1)

    r1 = around(shard)
    x0 = beside(shard)
    c0 = twin(shard)
    near = [twin(chosen[0]), beside(after(chosen[1], c0))]
    r2 = around(r1)
    cr1 = twin(r1)
    x1 = beside(after(r1, near[1]))
    l1 = back(after(shard, cr1))
    cx0 = twin(x0)
    x2 = beside(after(r2, cx0, cr1))
    cr2 = twin(r2)
    cx1 = twin(x1)
    x3 = beside(after(l1, cx1, cr2))
    far = [swapped(after(chosen[3], r2), "seq", 8), swapped(after(chosen[2], l1), "seq", 4)]
    cl1 = twin(l1)
    cx2 = twin(x2)
    early = [
        (shard, 0, 0, 0),
        (c0, 0, 0, 1),
        (r1, 1, 0, 0),
        (cr1, 1, 0, 1),
        (l1, 3, 0, 0),
        (cl1, 3, 0, 1),
        (r2, 2, 0, 0),
        (cr2, 2, 0, 1),
        (x0, 0, 1, 0),
        (cx0, 0, 1, 1),
        (x1, 1, 1, 0),
        (cx1, 1, 1, 1),
        (x2, 2, 1, 0),
        (cx2, 2, 1, 1),
    ]
    triple = assembled([piece for piece, *_ in early], [tuple(hops) for _, *hops in early])
    started = ahead(triple, own, gain)
    return triple, started, [x3, twin(after(x3, started, *far))], near + far[::-1]


def partner_rows(chosen):
    twin = swapped(chosen[0], "seq", 1)
    late = [after(block, twin) for block in chosen[1:-1]] + [chosen[-1]]
    return [twin] + [swapped(block, "seq", 2 << level) for level, block in enumerate(late)]


def per_device(resident, arriving, gain, triple, exit_matrix, lookup):
    first_in = resident[0]
    me = lax.axis_index("seq")
    levels = jnp.arange(8, dtype=jnp.int32)
    partner = jnp.bitwise_xor(me, jnp.left_shift(1, levels % LEVELS))
    wanted = jnp.broadcast_to(lookup[partner, levels % LEVELS][:, None], (8, 128))
    _, chosen = choose(wanted, first_in, first_in)
    if lax.axis_size("seq") == 16:
        triple, started, latest, fars = gathered(triple[0], chosen, first_in, gain)
    else:
        triple = lax.all_gather(triple[0], "seq", axis=0, tiled=True)
        started = ahead(triple, first_in, gain)
        latest = []
        fars = partner_rows(chosen)
    first_out = first_layer(triple, first_in, started, fars, gain, exit_matrix[0], latest)
    moved = from_behind(first_out, "section", 1)
    second_in, chosen = choose(wanted, moved, arriving)
    fars = partner_rows(chosen)
    return second_layer(triple, second_in, ahead(triple, second_in, gain), fars, gain, exit_matrix[0], latest, first_out)[:, None]


def solution(mesh):
    placed = (
        P("section", "seq", None),
        P("seq", None),
        P("section", None),
        P("section", "seq", None),
        P("section", None, None),
        P(),
    )
    return jax.shard_map(
        per_device,
        mesh=mesh,
        in_specs=placed,
        out_specs=P(None, "section", "seq", None),
        check_vma=False,
    )
```

```python
import functools
import math

import jax
import jax.numpy as jnp
from jax import lax
from jax.experimental import pallas as pl
from jax.experimental.pallas import tpu as pltpu
from jax.sharding import PartitionSpec as P

HEADS = 8
HEAD = 128
BLOCK = 64
LEVELS = 4
WIDE = 256
MIB = 1024 * 1024

epsilon = 1e-06

in_vmem = pl.BlockSpec(memory_space=pltpu.VMEM)
in_smem = pl.BlockSpec(memory_space=pltpu.SMEM)
anywhere = pl.BlockSpec(memory_space=pl.ANY)


def swapped(x, axis, mask):
    return lax.ppermute(x, axis, [(i, i ^ mask) for i in range(lax.axis_size(axis))])


def from_behind(block, axis, distance):
    devices = range(lax.axis_size(axis))
    route = [(i - distance, i) for i in devices if i - distance in devices]
    return lax.ppermute(block, axis, route)


def after(x, *others):
    return lax.optimization_barrier((x, *others))[0]


def row_norm(rows, gain):
    widened = rows.astype(jnp.float32)
    mean_square = jnp.mean(widened * widened, axis=-1, keepdims=True)
    return (widened * lax.rsqrt(mean_square + epsilon) * gain).astype(jnp.bfloat16)


def head_norm(one_head):
    mean_square = jnp.mean(one_head * one_head, axis=-1, keepdims=True)
    return (one_head * lax.rsqrt(mean_square + epsilon)).astype(jnp.bfloat16)


def choose_kernel(wanted, moved_ref, arriving_ref, own_ref, *chosen):
    first = lax.axis_index("section") == 0

    @pl.when(first)
    def _():
        own_ref[...] = arriving_ref[...]

    @pl.when(jnp.logical_not(first))
    def _():
        own_ref[...] = moved_ref[...]

    shape = chosen[0].shape
    for level in range(LEVELS):
        asked = jnp.broadcast_to(wanted[level : level + 1, :1], shape)
        block = own_ref[:BLOCK].astype(jnp.float32)
        for i in range(1, own_ref.shape[0] // BLOCK):
            block = jnp.where(asked == i, own_ref[i * BLOCK : (i + 1) * BLOCK].astype(jnp.float32), block)
        chosen[level][...] = block.astype(own_ref.dtype)


def choose(wanted, moved, arriving):
    rows, width = moved.shape
    block = jax.ShapeDtypeStruct((BLOCK, width), moved.dtype)
    own, *chosen = pl.pallas_call(
        choose_kernel,
        out_shape=[jax.ShapeDtypeStruct((rows, width), moved.dtype)] + [block] * LEVELS,
        in_specs=[in_vmem] * 3,
        out_specs=[in_vmem] * (1 + LEVELS),
        compiler_params=pltpu.CompilerParams(vmem_limit_bytes=4 * MIB),
    )(wanted, moved, arriving)
    return own, chosen


def origin(behind, beside, twin):
    me = lax.axis_index("seq")
    plane = me // 4
    spot = jnp.bitwise_and(jnp.bitwise_xor(plane, plane // 2) + 4 - behind, 3)
    plane = jnp.bitwise_xor(spot, spot // 2)
    return plane * 4 + jnp.bitwise_xor(lax.rem(me, 4), 2 * beside + twin)


def assemble_kernel(places, *refs):
    pieces, (triple, sem) = refs[:-2], refs[-2:]
    rows, width = pieces[0].shape
    copies = []
    for i, (piece, hops) in enumerate(zip(pieces, places)):
        spot = pl.multiple_of(origin(*hops) * rows, rows)
        copies.append(pltpu.make_async_copy(piece, triple.at[pl.ds(spot, rows), :], sem.at[i]))
        copies[-1].start()
    spot = pl.multiple_of(origin(3, 1, 0) // 2 * (2 * rows), 2 * rows)
    triple[pl.ds(spot, 2 * rows), :] = jnp.zeros((2 * rows, width), triple.dtype)
    for copy in copies:
        copy.wait()


def assembled(pieces, places):
    rows, width = pieces[0].shape
    return pl.pallas_call(
        functools.partial(assemble_kernel, places),
        out_shape=pltpu.VMEM((rows * lax.axis_size("seq"), width), pieces[0].dtype),
        in_specs=[anywhere] * len(pieces),
        out_specs=in_vmem,
        scratch_shapes=[pltpu.SemaphoreType.DMA((len(pieces),))],
        compiler_params=pltpu.CompilerParams(vmem_limit_bytes=8 * MIB),
        cost_estimate=pl.CostEstimate(flops=0, bytes_accessed=12_000_000, transcendentals=0),
    )(*pieces)


def ahead_kernel(first_column, triple, *refs):
    tokens, (gain_ref, out_ref, normed) = refs[:-3], refs[-3:]
    low = 0
    for part in tokens:
        high = low + part.shape[0]
        normed[low:high] = row_norm(part[...], gain_ref[...])
        low = high
    for start in range(0, out_ref.shape[1], WIDE):
        out_ref[:, start : start + WIDE] = jnp.dot(
            normed[...],
            triple[:, first_column + start : first_column + start + WIDE],
            preferred_element_type=jnp.float32,
        )


def ahead(triple, tokens, gain, first_column):
    rows = sum(part.shape[0] for part in tokens)
    width = tokens[0].shape[1]
    return pl.pallas_call(
        functools.partial(ahead_kernel, first_column),
        out_shape=pltpu.VMEM((rows, triple.shape[1] - first_column), jnp.float32),
        in_specs=[in_vmem] * (2 + len(tokens)),
        out_specs=in_vmem,
        scratch_shapes=[pltpu.VMEM((rows, width), jnp.bfloat16)],
        compiler_params=pltpu.CompilerParams(vmem_limit_bytes=4 * MIB),
        cost_estimate=pl.CostEstimate(flops=800_000_000, bytes_accessed=8_000_000, transcendentals=0),
    )(triple, *tokens, gain)


def attend(own_ref, started, far_started, fars, gain_ref, triple, exit_ref, latest, put, normed, queries, keys, values, attended, last):
    inner = HEADS * HEAD
    rows = own_ref.shape[0]
    far_rows = LEVELS * BLOCK
    gain = gain_ref[...]
    normed[:rows] = row_norm(own_ref[...], gain)
    for level in range(LEVELS):
        normed[rows + level * BLOCK : rows + (level + 1) * BLOCK] = row_norm(fars[level][...], gain)
    if latest:
        part = latest[0].shape[0]
        core = lax.rem(lax.axis_index("seq"), 2)
        last[pl.ds(pl.multiple_of(core * part, part), part), :] = latest[0][...]
        last[pl.ds(pl.multiple_of((1 - core) * part, part), part), :] = latest[1][...]
        spot = pl.multiple_of(origin(3, 1, 0) // 2 * (2 * part), 2 * part)
        late_columns = normed[:, pl.ds(spot, 2 * part)]

    def own_part(start):
        span = slice(start, start + WIDE)
        result = started[:, span]
        if latest:
            result += jnp.dot(late_columns[:rows], last[:, span], preferred_element_type=jnp.float32)
        return result

    def far_part(start):
        span = slice(start, start + WIDE)
        if far_started is None:
            result = jnp.dot(normed[rows:], triple[:, span], preferred_element_type=jnp.float32)
        else:
            result = far_started[:, start - inner : start - inner + WIDE]
        if latest:
            result += jnp.dot(late_columns[rows:], last[:, span], preferred_element_type=jnp.float32)
        return result

    for start in range(0, inner, WIDE):
        projected = own_part(start)
        for head in range(0, WIDE, HEAD):
            queries[:, start + head : start + head + HEAD] = head_norm(projected[:, head : head + HEAD])
    for start in range(0, inner, WIDE):
        near, far = own_part(inner + start), far_part(inner + start)
        for head in range(0, WIDE, HEAD):
            span = slice(start + head, start + head + HEAD)
            keys[:rows, span] = head_norm(near[:, head : head + HEAD])
            keys[rows:, span] = head_norm(far[:, head : head + HEAD])
    for start in range(0, inner, WIDE):
        span = slice(start, start + WIDE)
        values[:rows, span] = own_part(2 * inner + start).astype(jnp.bfloat16)
        values[rows:, span] = far_part(2 * inner + start).astype(jnp.bfloat16)
    reader = lax.broadcasted_iota(jnp.int32, (rows, rows), 0) // BLOCK
    column = lax.broadcasted_iota(jnp.int32, (rows, rows), 1) // BLOCK
    read = reader == column
    score_scale = HEAD ** (-0.5) * math.log2(math.e)
    spans = [slice(start, start + HEAD) for start in range(0, inner, HEAD)]
    scores = [
        lax.dot_general(
            queries[:, span], keys[:, span], (((1,), (1,)), ((), ())), preferred_element_type=jnp.float32
        )
        for span in spans
    ]
    weights = []
    for score in scores:
        exps = jnp.exp2(score * score_scale)
        exps = jnp.concatenate([jnp.where(read, exps[:, :rows], 0.0), exps[:, rows:]], axis=1)
        total = jnp.sum(exps, axis=-1, keepdims=True)
        weights.append((exps * (1.0 / total)).astype(jnp.bfloat16))
    for span, weight in zip(spans, weights):
        attended[:, span] = jnp.dot(weight, values[:, span], preferred_element_type=jnp.float32).astype(jnp.bfloat16)
    for start in range(0, own_ref.shape[1], WIDE):
        span = slice(start, start + WIDE)
        put[:, span] = (
            own_ref[:, span].astype(jnp.float32)
            + jnp.dot(attended[...], exit_ref[:, span], preferred_element_type=jnp.float32)
        ).astype(jnp.bfloat16)


def first_kernel(late, far_started, own_ref, started, *refs):
    fars, refs = refs[:LEVELS], refs[LEVELS:]
    gain_ref, exit_ref, *refs = refs
    latest, refs = refs[:late], refs[late:]
    out_ref, *scratch = refs
    attend(own_ref, started, far_started, fars, gain_ref, None, exit_ref, latest, out_ref, *scratch)


def second_kernel(late, triple, own_ref, started, *refs):
    fars, refs = refs[:LEVELS], refs[LEVELS:]
    gain_ref, exit_ref, *refs = refs
    latest, refs = refs[:late], refs[late:]
    first_ref, out_ref, result, sems, *scratch = refs
    early = pltpu.make_async_copy(first_ref, out_ref.at[0], sems.at[0])
    early.start()
    attend(own_ref, started, None, fars, gain_ref, triple, exit_ref, latest, result, *scratch)
    finish = pltpu.make_async_copy(result, out_ref.at[1], sems.at[1])
    finish.start()
    early.wait()
    finish.wait()


def scratch_of(rows, width, triple, latest):
    inner = HEADS * HEAD
    reach = rows + LEVELS * BLOCK
    late_rows = 2 * latest[0].shape[0] if latest else 16
    return [
        pltpu.VMEM((reach, width), jnp.bfloat16),
        pltpu.VMEM((rows, inner), jnp.bfloat16),
        pltpu.VMEM((reach, inner), jnp.bfloat16),
        pltpu.VMEM((reach, inner), jnp.bfloat16),
        pltpu.VMEM((rows, inner), jnp.bfloat16),
        pltpu.VMEM((late_rows, triple.shape[1]), jnp.bfloat16),
    ]


cost = pl.CostEstimate(flops=2_400_000_000, bytes_accessed=9_000_000, transcendentals=400_000)


def first_layer(far_started, own, started, fars, gain, exit_matrix, latest):
    return pl.pallas_call(
        functools.partial(first_kernel, len(latest)),
        out_shape=jax.ShapeDtypeStruct(own.shape, own.dtype),
        in_specs=[in_vmem] * (5 + LEVELS + len(latest)),
        out_specs=in_vmem,
        scratch_shapes=scratch_of(*own.shape, started, latest),
        compiler_params=pltpu.CompilerParams(vmem_limit_bytes=16 * MIB),
        cost_estimate=cost,
    )(far_started, own, started, *fars, gain, exit_matrix, *latest)


def second_layer(triple, own, started, fars, gain, exit_matrix, latest, first_out):
    return pl.pallas_call(
        functools.partial(second_kernel, len(latest)),
        out_shape=jax.ShapeDtypeStruct((2,) + own.shape, own.dtype),
        in_specs=[in_vmem] * (6 + LEVELS + len(latest)),
        out_specs=anywhere,
        scratch_shapes=[pltpu.VMEM(own.shape, own.dtype), pltpu.SemaphoreType.DMA((2,))]
        + scratch_of(*own.shape, triple, latest),
        compiler_params=pltpu.CompilerParams(vmem_limit_bytes=16 * MIB),
        cost_estimate=cost,
    )(triple, own, started, *fars, gain, exit_matrix, *latest, first_out)


def gathered(shard, chosen, own, gain):
    ring = [0, 1, 3, 2]
    onward = {ring[i]: ring[(i + 1) % 4] for i in range(4)}

    def around(x):
        return lax.ppermute(x, "seq", [(i, onward[i // 4] * 4 + i % 4) for i in range(16)])

    def back(x):
        return lax.ppermute(x, "seq", [(onward[i // 4] * 4 + i % 4, i) for i in range(16)])

    def beside(x):
        return swapped(x, "seq", 2)

    def twin(x):
        return swapped(x, "seq", 1)

    r1 = around(shard)
    x0 = beside(shard)
    near = [twin(chosen[0]), beside(chosen[1])]
    c0 = twin(after(shard, near[0]))
    r2 = around(after(r1, near[0]))
    cr1 = twin(r1)
    x1 = beside(after(r1, near[1]))
    l1 = back(after(shard, cr1))
    cx0 = twin(x0)
    x2 = beside(after(r2, cx0, cr1))
    cr2 = twin(r2)
    cx1 = twin(x1)
    x3 = beside(after(l1, cx1, cr2))
    far = [swapped(after(chosen[3], r2), "seq", 8), swapped(after(chosen[2], l1), "seq", 4)]
    cl1 = twin(l1)
    cx2 = twin(x2)
    early = [
        (shard, 0, 0, 0),
        (c0, 0, 0, 1),
        (r1, 1, 0, 0),
        (cr1, 1, 0, 1),
        (l1, 3, 0, 0),
        (cl1, 3, 0, 1),
        (r2, 2, 0, 0),
        (cr2, 2, 0, 1),
        (x0, 0, 1, 0),
        (cx0, 0, 1, 1),
        (x1, 1, 1, 0),
        (cx1, 1, 1, 1),
        (x2, 2, 1, 0),
        (cx2, 2, 1, 1),
    ]
    triple = assembled([piece for piece, *_ in early], [tuple(hops) for _, *hops in early])
    fars = near + far[::-1]
    started = ahead(triple, [own], gain, 0)
    far_started = ahead(triple, fars, gain, HEADS * HEAD)
    return triple, started, far_started, [x3, twin(after(x3, started, *far))], fars


def partner_rows(chosen):
    twin = swapped(chosen[0], "seq", 1)
    late = [after(block, twin) for block in chosen[1:-1]] + [chosen[-1]]
    return [twin] + [swapped(block, "seq", 2 << level) for level, block in enumerate(late)]


def per_device(resident, arriving, gain, triple, exit_matrix, lookup):
    first_in = resident[0]
    me = lax.axis_index("seq")
    levels = jnp.arange(8, dtype=jnp.int32)
    partner = jnp.bitwise_xor(me, jnp.left_shift(1, levels % LEVELS))
    wanted = jnp.broadcast_to(lookup[partner, levels % LEVELS][:, None], (8, 128))
    _, chosen = choose(wanted, first_in, first_in)
    if lax.axis_size("seq") == 16:
        triple, started, far_started, latest, fars = gathered(triple[0], chosen, first_in, gain)
    else:
        triple = lax.all_gather(triple[0], "seq", axis=0, tiled=True)
        fars = partner_rows(chosen)
        started = ahead(triple, [first_in], gain, 0)
        far_started = ahead(triple, fars, gain, HEADS * HEAD)
        latest = []
    first_out = first_layer(far_started, first_in, started, fars, gain, exit_matrix[0], latest)
    moved = from_behind(first_out, "section", 1)
    second_in, chosen = choose(wanted, moved, arriving)
    fars = partner_rows(chosen)
    return second_layer(triple, second_in, ahead(triple, [second_in], gain, 0), fars, gain, exit_matrix[0], latest, first_out)[:, None]


def solution(mesh):
    placed = (
        P("section", "seq", None),
        P("seq", None),
        P("section", None),
        P("section", "seq", None),
        P("section", None, None),
        P(),
    )
    return jax.shard_map(
        per_device,
        mesh=mesh,
        in_specs=placed,
        out_specs=P(None, "section", "seq", None),
        check_vma=False,
    )
```

```python
import functools
import math

import jax
import jax.numpy as jnp
from jax import lax
from jax.experimental import pallas as pl
from jax.experimental.pallas import tpu as pltpu
from jax.sharding import PartitionSpec as P

HEADS = 8
HEAD = 128
BLOCK = 64
LEVELS = 4
WIDE = 256
MIB = 1024 * 1024

epsilon = 1e-06

in_vmem = pl.BlockSpec(memory_space=pltpu.VMEM)
in_smem = pl.BlockSpec(memory_space=pltpu.SMEM)
anywhere = pl.BlockSpec(memory_space=pl.ANY)


def swapped(x, axis, mask):
    return lax.ppermute(x, axis, [(i, i ^ mask) for i in range(lax.axis_size(axis))])


def from_behind(block, axis, distance):
    devices = range(lax.axis_size(axis))
    route = [(i - distance, i) for i in devices if i - distance in devices]
    return lax.ppermute(block, axis, route)


def after(x, *others):
    return lax.optimization_barrier((x, *others))[0]


def row_norm(rows, gain):
    widened = rows.astype(jnp.float32)
    mean_square = jnp.mean(widened * widened, axis=-1, keepdims=True)
    return (widened * lax.rsqrt(mean_square + epsilon) * gain).astype(jnp.bfloat16)


def head_norm(one_head):
    mean_square = jnp.mean(one_head * one_head, axis=-1, keepdims=True)
    return (one_head * lax.rsqrt(mean_square + epsilon)).astype(jnp.bfloat16)


def choose_kernel(wanted, moved_ref, arriving_ref, own_ref, *chosen):
    first = lax.axis_index("section") == 0

    @pl.when(first)
    def _():
        own_ref[...] = arriving_ref[...]

    @pl.when(jnp.logical_not(first))
    def _():
        own_ref[...] = moved_ref[...]

    shape = chosen[0].shape
    for level in range(LEVELS):
        asked = jnp.broadcast_to(wanted[level : level + 1, :1], shape)
        block = own_ref[:BLOCK].astype(jnp.float32)
        for i in range(1, own_ref.shape[0] // BLOCK):
            block = jnp.where(asked == i, own_ref[i * BLOCK : (i + 1) * BLOCK].astype(jnp.float32), block)
        chosen[level][...] = block.astype(own_ref.dtype)


def choose(wanted, moved, arriving):
    rows, width = moved.shape
    block = jax.ShapeDtypeStruct((BLOCK, width), moved.dtype)
    own, *chosen = pl.pallas_call(
        choose_kernel,
        out_shape=[jax.ShapeDtypeStruct((rows, width), moved.dtype)] + [block] * LEVELS,
        in_specs=[in_vmem] * 3,
        out_specs=[in_vmem] * (1 + LEVELS),
        compiler_params=pltpu.CompilerParams(vmem_limit_bytes=4 * MIB),
    )(wanted, moved, arriving)
    return own, chosen


def origin(behind, beside, twin):
    me = lax.axis_index("seq")
    plane = me // 4
    spot = jnp.bitwise_and(jnp.bitwise_xor(plane, plane // 2) + 4 - behind, 3)
    plane = jnp.bitwise_xor(spot, spot // 2)
    return plane * 4 + jnp.bitwise_xor(lax.rem(me, 4), 2 * beside + twin)


def assemble_kernel(places, *refs):
    pieces, (triple, sem) = refs[:-2], refs[-2:]
    rows, width = pieces[0].shape
    copies = []
    for i, (piece, hops) in enumerate(zip(pieces, places)):
        spot = pl.multiple_of(origin(*hops) * rows, rows)
        copies.append(pltpu.make_async_copy(piece, triple.at[pl.ds(spot, rows), :], sem.at[i]))
        copies[-1].start()
    spot = pl.multiple_of(origin(3, 1, 0) // 2 * (2 * rows), 2 * rows)
    triple[pl.ds(spot, 2 * rows), :] = jnp.zeros((2 * rows, width), triple.dtype)
    for copy in copies:
        copy.wait()


def assembled(pieces, places):
    rows, width = pieces[0].shape
    return pl.pallas_call(
        functools.partial(assemble_kernel, places),
        out_shape=pltpu.VMEM((rows * lax.axis_size("seq"), width), pieces[0].dtype),
        in_specs=[anywhere] * len(pieces),
        out_specs=in_vmem,
        scratch_shapes=[pltpu.SemaphoreType.DMA((len(pieces),))],
        compiler_params=pltpu.CompilerParams(vmem_limit_bytes=8 * MIB),
        cost_estimate=pl.CostEstimate(flops=0, bytes_accessed=12_000_000, transcendentals=0),
    )(*pieces)


def ahead_kernel(first_column, triple, *refs):
    tokens, (gain_ref, out_ref, normed) = refs[:-3], refs[-3:]
    low = 0
    for part in tokens:
        high = low + part.shape[0]
        normed[low:high] = row_norm(part[...], gain_ref[...])
        low = high
    for start in range(0, out_ref.shape[1], WIDE):
        out_ref[:, start : start + WIDE] = jnp.dot(
            normed[...],
            triple[:, first_column + start : first_column + start + WIDE],
            preferred_element_type=jnp.float32,
        )


def ahead(triple, tokens, gain, first_column):
    rows = sum(part.shape[0] for part in tokens)
    width = tokens[0].shape[1]
    return pl.pallas_call(
        functools.partial(ahead_kernel, first_column),
        out_shape=pltpu.VMEM((rows, triple.shape[1] - first_column), jnp.float32),
        in_specs=[in_vmem] * (2 + len(tokens)),
        out_specs=in_vmem,
        scratch_shapes=[pltpu.VMEM((rows, width), jnp.bfloat16)],
        compiler_params=pltpu.CompilerParams(vmem_limit_bytes=4 * MIB),
        cost_estimate=pl.CostEstimate(flops=800_000_000, bytes_accessed=8_000_000, transcendentals=0),
    )(triple, *tokens, gain)


def attend(own_ref, started, far_started, fars, gain_ref, triple, exit_ref, latest, put, normed, queries, keys, values, attended, last):
    inner = HEADS * HEAD
    rows = own_ref.shape[0]
    far_rows = LEVELS * BLOCK
    gain = gain_ref[...]
    normed[:rows] = row_norm(own_ref[...], gain)
    for level in range(LEVELS):
        normed[rows + level * BLOCK : rows + (level + 1) * BLOCK] = row_norm(fars[level][...], gain)
    if latest:
        part = latest[0].shape[0]
        core = lax.rem(lax.axis_index("seq"), 2)
        last[pl.ds(pl.multiple_of(core * part, part), part), :] = latest[0][...]
        last[pl.ds(pl.multiple_of((1 - core) * part, part), part), :] = latest[1][...]
        spot = pl.multiple_of(origin(3, 1, 0) // 2 * (2 * part), 2 * part)
        late_columns = normed[:, pl.ds(spot, 2 * part)]

    def own_part(start):
        span = slice(start, start + WIDE)
        result = started[:rows, span]
        if latest:
            result += jnp.dot(late_columns[:rows], last[:, span], preferred_element_type=jnp.float32)
        return result

    def far_part(start):
        span = slice(start, start + WIDE)
        if far_started is None:
            ready = started.shape[0]
            result = jnp.dot(normed[ready:], triple[:, span], preferred_element_type=jnp.float32)
            if ready > rows:
                result = jnp.concatenate([started[rows:, span], result], axis=0)
        else:
            result = far_started[:, start - inner : start - inner + WIDE]
        if latest:
            result += jnp.dot(late_columns[rows:], last[:, span], preferred_element_type=jnp.float32)
        return result

    for start in range(0, inner, WIDE):
        projected = own_part(start)
        for head in range(0, WIDE, HEAD):
            queries[:, start + head : start + head + HEAD] = head_norm(projected[:, head : head + HEAD])
    for start in range(0, inner, WIDE):
        near, far = own_part(inner + start), far_part(inner + start)
        for head in range(0, WIDE, HEAD):
            span = slice(start + head, start + head + HEAD)
            keys[:rows, span] = head_norm(near[:, head : head + HEAD])
            keys[rows:, span] = head_norm(far[:, head : head + HEAD])
    for start in range(0, inner, WIDE):
        span = slice(start, start + WIDE)
        values[:rows, span] = own_part(2 * inner + start).astype(jnp.bfloat16)
        values[rows:, span] = far_part(2 * inner + start).astype(jnp.bfloat16)
    reader = lax.broadcasted_iota(jnp.int32, (rows, rows), 0) // BLOCK
    column = lax.broadcasted_iota(jnp.int32, (rows, rows), 1) // BLOCK
    read = reader == column
    score_scale = HEAD ** (-0.5) * math.log2(math.e)
    spans = [slice(start, start + HEAD) for start in range(0, inner, HEAD)]
    scores = [
        lax.dot_general(
            queries[:, span], keys[:, span], (((1,), (1,)), ((), ())), preferred_element_type=jnp.float32
        )
        for span in spans
    ]
    weights = []
    for score in scores:
        exps = jnp.exp2(score * score_scale)
        exps = jnp.concatenate([jnp.where(read, exps[:, :rows], 0.0), exps[:, rows:]], axis=1)
        total = jnp.sum(exps, axis=-1, keepdims=True)
        weights.append((exps * (1.0 / total)).astype(jnp.bfloat16))
    for span, weight in zip(spans, weights):
        attended[:, span] = jnp.dot(weight, values[:, span], preferred_element_type=jnp.float32).astype(jnp.bfloat16)
    for start in range(0, own_ref.shape[1], WIDE):
        span = slice(start, start + WIDE)
        put[:, span] = (
            own_ref[:, span].astype(jnp.float32)
            + jnp.dot(attended[...], exit_ref[:, span], preferred_element_type=jnp.float32)
        ).astype(jnp.bfloat16)


def first_kernel(late, far_started, own_ref, started, *refs):
    fars, refs = refs[:LEVELS], refs[LEVELS:]
    gain_ref, exit_ref, *refs = refs
    latest, refs = refs[:late], refs[late:]
    out_ref, *scratch = refs
    attend(own_ref, started, far_started, fars, gain_ref, None, exit_ref, latest, out_ref, *scratch)


def second_kernel(late, triple, own_ref, started, *refs):
    fars, refs = refs[:LEVELS], refs[LEVELS:]
    gain_ref, exit_ref, *refs = refs
    latest, refs = refs[:late], refs[late:]
    first_ref, out_ref, result, sems, *scratch = refs
    early = pltpu.make_async_copy(first_ref, out_ref.at[0], sems.at[0])
    early.start()
    attend(own_ref, started, None, fars, gain_ref, triple, exit_ref, latest, result, *scratch)
    finish = pltpu.make_async_copy(result, out_ref.at[1], sems.at[1])
    finish.start()
    early.wait()
    finish.wait()


def scratch_of(rows, width, triple, latest):
    inner = HEADS * HEAD
    reach = rows + LEVELS * BLOCK
    late_rows = 2 * latest[0].shape[0] if latest else 16
    return [
        pltpu.VMEM((reach, width), jnp.bfloat16),
        pltpu.VMEM((rows, inner), jnp.bfloat16),
        pltpu.VMEM((reach, inner), jnp.bfloat16),
        pltpu.VMEM((reach, inner), jnp.bfloat16),
        pltpu.VMEM((rows, inner), jnp.bfloat16),
        pltpu.VMEM((late_rows, triple.shape[1]), jnp.bfloat16),
    ]


cost = pl.CostEstimate(flops=2_400_000_000, bytes_accessed=9_000_000, transcendentals=400_000)


def first_layer(far_started, own, started, fars, gain, exit_matrix, latest):
    return pl.pallas_call(
        functools.partial(first_kernel, len(latest)),
        out_shape=jax.ShapeDtypeStruct(own.shape, own.dtype),
        in_specs=[in_vmem] * (5 + LEVELS + len(latest)),
        out_specs=in_vmem,
        scratch_shapes=scratch_of(*own.shape, started, latest),
        compiler_params=pltpu.CompilerParams(vmem_limit_bytes=16 * MIB),
        cost_estimate=cost,
    )(far_started, own, started, *fars, gain, exit_matrix, *latest)


def second_layer(triple, own, started, fars, gain, exit_matrix, latest, first_out):
    return pl.pallas_call(
        functools.partial(second_kernel, len(latest)),
        out_shape=jax.ShapeDtypeStruct((2,) + own.shape, own.dtype),
        in_specs=[in_vmem] * (6 + LEVELS + len(latest)),
        out_specs=anywhere,
        scratch_shapes=[pltpu.VMEM(own.shape, own.dtype), pltpu.SemaphoreType.DMA((2,))]
        + scratch_of(*own.shape, triple, latest),
        compiler_params=pltpu.CompilerParams(vmem_limit_bytes=16 * MIB),
        cost_estimate=cost,
    )(triple, own, started, *fars, gain, exit_matrix, *latest, first_out)


def gathered(shard, chosen, own, gain):
    ring = [0, 1, 3, 2]
    onward = {ring[i]: ring[(i + 1) % 4] for i in range(4)}

    def around(x):
        return lax.ppermute(x, "seq", [(i, onward[i // 4] * 4 + i % 4) for i in range(16)])

    def back(x):
        return lax.ppermute(x, "seq", [(onward[i // 4] * 4 + i % 4, i) for i in range(16)])

    def beside(x):
        return swapped(x, "seq", 2)

    def twin(x):
        return swapped(x, "seq", 1)

    r1 = around(shard)
    x0 = beside(shard)
    near = [twin(chosen[0]), beside(chosen[1])]
    r2 = around(after(r1, near[0]))
    cr1 = twin(r1)
    x1 = beside(after(r1, near[1]))
    l1 = back(after(shard, cr1))
    cx0 = twin(x0)
    c0 = twin(after(shard, r2))
    x2 = beside(after(r2, cx0, cr1))
    cr2 = twin(r2)
    cx1 = twin(x1)
    x3 = beside(after(l1, cx1, cr2))
    far = [swapped(after(chosen[3], r2), "seq", 8), swapped(after(chosen[2], l1), "seq", 4)]
    cl1 = twin(l1)
    cx2 = twin(x2)
    early = [
        (shard, 0, 0, 0),
        (c0, 0, 0, 1),
        (r1, 1, 0, 0),
        (cr1, 1, 0, 1),
        (l1, 3, 0, 0),
        (cl1, 3, 0, 1),
        (r2, 2, 0, 0),
        (cr2, 2, 0, 1),
        (x0, 0, 1, 0),
        (cx0, 0, 1, 1),
        (x1, 1, 1, 0),
        (cx1, 1, 1, 1),
        (x2, 2, 1, 0),
        (cx2, 2, 1, 1),
    ]
    triple = assembled([piece for piece, *_ in early], [tuple(hops) for _, *hops in early])
    fars = near + far[::-1]
    started = ahead(triple, [own], gain, 0)
    far_started = ahead(triple, fars, gain, HEADS * HEAD)
    return triple, started, far_started, [x3, twin(after(x3, started, *far))], fars


def partner_rows(chosen):
    twin = swapped(chosen[0], "seq", 1)
    late = [after(block, twin) for block in chosen[1:-1]] + [chosen[-1]]
    return [twin] + [swapped(block, "seq", 2 << level) for level, block in enumerate(late)]


def per_device(resident, arriving, gain, triple, exit_matrix, lookup):
    first_in = resident[0]
    me = lax.axis_index("seq")
    levels = jnp.arange(8, dtype=jnp.int32)
    partner = jnp.bitwise_xor(me, jnp.left_shift(1, levels % LEVELS))
    wanted = jnp.broadcast_to(lookup[partner, levels % LEVELS][:, None], (8, 128))
    _, chosen = choose(wanted, first_in, first_in)
    if lax.axis_size("seq") == 16:
        triple, started, far_started, latest, fars = gathered(triple[0], chosen, first_in, gain)
    else:
        triple = lax.all_gather(triple[0], "seq", axis=0, tiled=True)
        fars = partner_rows(chosen)
        started = ahead(triple, [first_in], gain, 0)
        far_started = ahead(triple, fars, gain, HEADS * HEAD)
        latest = []
    first_out = first_layer(far_started, first_in, started, fars, gain, exit_matrix[0], latest)
    moved = from_behind(first_out, "section", 1)
    second_in, chosen = choose(wanted, moved, arriving)
    fars = partner_rows(chosen)
    return second_layer(triple, second_in, ahead(triple, [second_in, fars[0]], gain, 0), fars, gain, exit_matrix[0], latest, first_out)[:, None]


def solution(mesh):
    placed = (
        P("section", "seq", None),
        P("seq", None),
        P("section", None),
        P("section", "seq", None),
        P("section", None, None),
        P(),
    )
    return jax.shard_map(
        per_device,
        mesh=mesh,
        in_specs=placed,
        out_specs=P(None, "section", "seq", None),
        check_vma=False,
    )
```

```python
import functools
import math

import jax
import jax.numpy as jnp
from jax import lax
from jax.experimental import pallas as pl
from jax.experimental.pallas import tpu as pltpu
from jax.sharding import PartitionSpec as P

HEADS = 8
HEAD = 128
BLOCK = 64
LEVELS = 4
WIDE = 512
MIB = 1024 * 1024

epsilon = 1e-06

in_vmem = pl.BlockSpec(memory_space=pltpu.VMEM)
in_smem = pl.BlockSpec(memory_space=pltpu.SMEM)
anywhere = pl.BlockSpec(memory_space=pl.ANY)


def swapped(x, axis, mask):
    return lax.ppermute(x, axis, [(i, i ^ mask) for i in range(lax.axis_size(axis))])


def from_behind(block, axis, distance):
    devices = range(lax.axis_size(axis))
    route = [(i - distance, i) for i in devices if i - distance in devices]
    return lax.ppermute(block, axis, route)


def after(x, *others):
    return lax.optimization_barrier((x, *others))[0]


def row_norm(rows, gain):
    widened = rows.astype(jnp.float32)
    mean_square = jnp.mean(widened * widened, axis=-1, keepdims=True)
    return (widened * lax.rsqrt(mean_square + epsilon) * gain).astype(jnp.bfloat16)


def head_norm(one_head):
    mean_square = jnp.mean(one_head * one_head, axis=-1, keepdims=True)
    return (one_head * lax.rsqrt(mean_square + epsilon)).astype(jnp.bfloat16)


def choose_kernel(wanted, moved_ref, arriving_ref, own_ref, *chosen):
    first = lax.axis_index("section") == 0

    @pl.when(first)
    def _():
        own_ref[...] = arriving_ref[...]

    @pl.when(jnp.logical_not(first))
    def _():
        own_ref[...] = moved_ref[...]

    shape = chosen[0].shape
    for level in range(LEVELS):
        asked = jnp.broadcast_to(wanted[level : level + 1, :1], shape)
        block = own_ref[:BLOCK].astype(jnp.float32)
        for i in range(1, own_ref.shape[0] // BLOCK):
            block = jnp.where(asked == i, own_ref[i * BLOCK : (i + 1) * BLOCK].astype(jnp.float32), block)
        chosen[level][...] = block.astype(own_ref.dtype)


def choose(wanted, moved, arriving):
    rows, width = moved.shape
    block = jax.ShapeDtypeStruct((BLOCK, width), moved.dtype)
    own, *chosen = pl.pallas_call(
        choose_kernel,
        out_shape=[jax.ShapeDtypeStruct((rows, width), moved.dtype)] + [block] * LEVELS,
        in_specs=[in_vmem] * 3,
        out_specs=[in_vmem] * (1 + LEVELS),
        compiler_params=pltpu.CompilerParams(vmem_limit_bytes=4 * MIB),
    )(wanted, moved, arriving)
    return own, chosen


def origin(behind, beside, twin):
    me = lax.axis_index("seq")
    plane = me // 4
    spot = jnp.bitwise_and(jnp.bitwise_xor(plane, plane // 2) + 4 - behind, 3)
    plane = jnp.bitwise_xor(spot, spot // 2)
    return plane * 4 + jnp.bitwise_xor(lax.rem(me, 4), 2 * beside + twin)


def assemble_kernel(places, *refs):
    pieces, (triple, sem) = refs[:-2], refs[-2:]
    rows, width = pieces[0].shape
    copies = []
    for i, (piece, hops) in enumerate(zip(pieces, places)):
        spot = pl.multiple_of(origin(*hops) * rows, rows)
        copies.append(pltpu.make_async_copy(piece, triple.at[pl.ds(spot, rows), :], sem.at[i]))
        copies[-1].start()
    spot = pl.multiple_of(origin(3, 1, 0) // 2 * (2 * rows), 2 * rows)
    triple[pl.ds(spot, 2 * rows), :] = jnp.zeros((2 * rows, width), triple.dtype)
    for copy in copies:
        copy.wait()


def assembled(pieces, places):
    rows, width = pieces[0].shape
    return pl.pallas_call(
        functools.partial(assemble_kernel, places),
        out_shape=pltpu.VMEM((rows * lax.axis_size("seq"), width), pieces[0].dtype),
        in_specs=[anywhere] * len(pieces),
        out_specs=in_vmem,
        scratch_shapes=[pltpu.SemaphoreType.DMA((len(pieces),))],
        compiler_params=pltpu.CompilerParams(vmem_limit_bytes=8 * MIB),
        cost_estimate=pl.CostEstimate(flops=0, bytes_accessed=12_000_000, transcendentals=0),
    )(*pieces)


def ahead_kernel(first_column, triple, *refs):
    tokens, (gain_ref, out_ref, normed) = refs[:-3], refs[-3:]
    low = 0
    for part in tokens:
        high = low + part.shape[0]
        normed[low:high] = row_norm(part[...], gain_ref[...])
        low = high
    for start in range(0, out_ref.shape[1], WIDE):
        out_ref[:, start : start + WIDE] = jnp.dot(
            normed[...],
            triple[:, first_column + start : first_column + start + WIDE],
            preferred_element_type=jnp.float32,
        )


def ahead(triple, tokens, gain, first_column):
    rows = sum(part.shape[0] for part in tokens)
    width = tokens[0].shape[1]
    return pl.pallas_call(
        functools.partial(ahead_kernel, first_column),
        out_shape=pltpu.VMEM((rows, triple.shape[1] - first_column), jnp.float32),
        in_specs=[in_vmem] * (2 + len(tokens)),
        out_specs=in_vmem,
        scratch_shapes=[pltpu.VMEM((rows, width), jnp.bfloat16)],
        compiler_params=pltpu.CompilerParams(vmem_limit_bytes=4 * MIB),
        cost_estimate=pl.CostEstimate(flops=800_000_000, bytes_accessed=8_000_000, transcendentals=0),
    )(triple, *tokens, gain)


def attend(own_ref, started, far_started, fars, gain_ref, triple, exit_ref, latest, put, normed, queries, keys, values, attended, last):
    inner = HEADS * HEAD
    rows = own_ref.shape[0]
    far_rows = LEVELS * BLOCK
    gain = gain_ref[...]
    normed[:rows] = row_norm(own_ref[...], gain)
    for level in range(LEVELS):
        normed[rows + level * BLOCK : rows + (level + 1) * BLOCK] = row_norm(fars[level][...], gain)
    if latest:
        part = latest[0].shape[0]
        core = lax.rem(lax.axis_index("seq"), 2)
        last[pl.ds(pl.multiple_of(core * part, part), part), :] = latest[0][...]
        last[pl.ds(pl.multiple_of((1 - core) * part, part), part), :] = latest[1][...]
        spot = pl.multiple_of(origin(3, 1, 0) // 2 * (2 * part), 2 * part)
        late_columns = normed[:, pl.ds(spot, 2 * part)]

    def own_part(start):
        span = slice(start, start + WIDE)
        result = started[:rows, span]
        if latest:
            result += jnp.dot(late_columns[:rows], last[:, span], preferred_element_type=jnp.float32)
        return result

    def far_part(start):
        span = slice(start, start + WIDE)
        if far_started is None:
            ready = started.shape[0]
            result = jnp.dot(normed[ready:], triple[:, span], preferred_element_type=jnp.float32)
            if ready > rows:
                result = jnp.concatenate([started[rows:, span], result], axis=0)
        else:
            result = far_started[:, start - inner : start - inner + WIDE]
        if latest:
            result += jnp.dot(late_columns[rows:], last[:, span], preferred_element_type=jnp.float32)
        return result

    for start in range(0, inner, WIDE):
        projected = own_part(start)
        for head in range(0, WIDE, HEAD):
            queries[:, start + head : start + head + HEAD] = head_norm(projected[:, head : head + HEAD])
    for start in range(0, inner, WIDE):
        near, far = own_part(inner + start), far_part(inner + start)
        for head in range(0, WIDE, HEAD):
            span = slice(start + head, start + head + HEAD)
            keys[:rows, span] = head_norm(near[:, head : head + HEAD])
            keys[rows:, span] = head_norm(far[:, head : head + HEAD])
    for start in range(0, inner, WIDE):
        span = slice(start, start + WIDE)
        values[:rows, span] = own_part(2 * inner + start).astype(jnp.bfloat16)
        values[rows:, span] = far_part(2 * inner + start).astype(jnp.bfloat16)
    reader = lax.broadcasted_iota(jnp.int32, (rows, rows), 0) // BLOCK
    column = lax.broadcasted_iota(jnp.int32, (rows, rows), 1) // BLOCK
    read = reader == column
    score_scale = HEAD ** (-0.5) * math.log2(math.e)
    spans = [slice(start, start + HEAD) for start in range(0, inner, HEAD)]
    scores = [
        lax.dot_general(
            queries[:, span], keys[:, span], (((1,), (1,)), ((), ())), preferred_element_type=jnp.float32
        )
        for span in spans
    ]
    weights = []
    for score in scores:
        exps = jnp.exp2(score * score_scale)
        exps = jnp.concatenate([jnp.where(read, exps[:, :rows], 0.0), exps[:, rows:]], axis=1)
        total = jnp.sum(exps, axis=-1, keepdims=True)
        weights.append((exps * (1.0 / total)).astype(jnp.bfloat16))
    for span, weight in zip(spans, weights):
        attended[:, span] = jnp.dot(weight, values[:, span], preferred_element_type=jnp.float32).astype(jnp.bfloat16)
    for start in range(0, own_ref.shape[1], WIDE):
        span = slice(start, start + WIDE)
        put[:, span] = (
            own_ref[:, span].astype(jnp.float32)
            + jnp.dot(attended[...], exit_ref[:, span], preferred_element_type=jnp.float32)
        ).astype(jnp.bfloat16)


def first_kernel(late, far_started, own_ref, started, *refs):
    fars, refs = refs[:LEVELS], refs[LEVELS:]
    gain_ref, exit_ref, *refs = refs
    latest, refs = refs[:late], refs[late:]
    out_ref, *scratch = refs
    attend(own_ref, started, far_started, fars, gain_ref, None, exit_ref, latest, out_ref, *scratch)


def second_kernel(late, triple, own_ref, started, *refs):
    fars, refs = refs[:LEVELS], refs[LEVELS:]
    gain_ref, exit_ref, *refs = refs
    latest, refs = refs[:late], refs[late:]
    first_ref, out_ref, result, sems, *scratch = refs
    early = pltpu.make_async_copy(first_ref, out_ref.at[0], sems.at[0])
    early.start()
    attend(own_ref, started, None, fars, gain_ref, triple, exit_ref, latest, result, *scratch)
    finish = pltpu.make_async_copy(result, out_ref.at[1], sems.at[1])
    finish.start()
    early.wait()
    finish.wait()


def scratch_of(rows, width, triple, latest):
    inner = HEADS * HEAD
    reach = rows + LEVELS * BLOCK
    late_rows = 2 * latest[0].shape[0] if latest else 16
    return [
        pltpu.VMEM((reach, width), jnp.bfloat16),
        pltpu.VMEM((rows, inner), jnp.bfloat16),
        pltpu.VMEM((reach, inner), jnp.bfloat16),
        pltpu.VMEM((reach, inner), jnp.bfloat16),
        pltpu.VMEM((rows, inner), jnp.bfloat16),
        pltpu.VMEM((late_rows, triple.shape[1]), jnp.bfloat16),
    ]


cost = pl.CostEstimate(flops=2_400_000_000, bytes_accessed=9_000_000, transcendentals=400_000)


def first_layer(far_started, own, started, fars, gain, exit_matrix, latest):
    return pl.pallas_call(
        functools.partial(first_kernel, len(latest)),
        out_shape=jax.ShapeDtypeStruct(own.shape, own.dtype),
        in_specs=[in_vmem] * (5 + LEVELS + len(latest)),
        out_specs=in_vmem,
        scratch_shapes=scratch_of(*own.shape, started, latest),
        compiler_params=pltpu.CompilerParams(vmem_limit_bytes=16 * MIB),
        cost_estimate=cost,
    )(far_started, own, started, *fars, gain, exit_matrix, *latest)


def second_layer(triple, own, started, fars, gain, exit_matrix, latest, first_out):
    return pl.pallas_call(
        functools.partial(second_kernel, len(latest)),
        out_shape=jax.ShapeDtypeStruct((2,) + own.shape, own.dtype),
        in_specs=[in_vmem] * (6 + LEVELS + len(latest)),
        out_specs=anywhere,
        scratch_shapes=[pltpu.VMEM(own.shape, own.dtype), pltpu.SemaphoreType.DMA((2,))]
        + scratch_of(*own.shape, triple, latest),
        compiler_params=pltpu.CompilerParams(vmem_limit_bytes=16 * MIB),
        cost_estimate=cost,
    )(triple, own, started, *fars, gain, exit_matrix, *latest, first_out)


def gathered(shard, chosen, own, gain):
    ring = [0, 1, 3, 2]
    onward = {ring[i]: ring[(i + 1) % 4] for i in range(4)}

    def around(x):
        return lax.ppermute(x, "seq", [(i, onward[i // 4] * 4 + i % 4) for i in range(16)])

    def back(x):
        return lax.ppermute(x, "seq", [(onward[i // 4] * 4 + i % 4, i) for i in range(16)])

    def beside(x):
        return swapped(x, "seq", 2)

    def twin(x):
        return swapped(x, "seq", 1)

    r1 = around(shard)
    x0 = beside(shard)
    near = [twin(chosen[0]), beside(chosen[1])]
    r2 = around(after(r1, near[0]))
    cr1 = twin(r1)
    x1 = beside(after(r1, near[1]))
    l1 = back(after(shard, cr1))
    cx0 = twin(x0)
    c0 = twin(after(shard, r2))
    x2 = beside(after(r2, cx0, cr1))
    cr2 = twin(r2)
    cx1 = twin(x1)
    x3 = beside(after(l1, cx1, cr2))
    far = [swapped(after(chosen[3], r2), "seq", 8), swapped(after(chosen[2], l1), "seq", 4)]
    cl1 = twin(l1)
    cx2 = twin(x2)
    early = [
        (shard, 0, 0, 0),
        (c0, 0, 0, 1),
        (r1, 1, 0, 0),
        (cr1, 1, 0, 1),
        (l1, 3, 0, 0),
        (cl1, 3, 0, 1),
        (r2, 2, 0, 0),
        (cr2, 2, 0, 1),
        (x0, 0, 1, 0),
        (cx0, 0, 1, 1),
        (x1, 1, 1, 0),
        (cx1, 1, 1, 1),
        (x2, 2, 1, 0),
        (cx2, 2, 1, 1),
    ]
    triple = assembled([piece for piece, *_ in early], [tuple(hops) for _, *hops in early])
    fars = near + far[::-1]
    started = ahead(triple, [own], gain, 0)
    far_started = ahead(triple, fars, gain, HEADS * HEAD)
    return triple, started, far_started, [x3, twin(after(x3, started, *far))], fars


def partner_rows(chosen):
    twin = swapped(chosen[0], "seq", 1)
    late = [after(block, twin) for block in chosen[1:-1]] + [chosen[-1]]
    return [twin] + [swapped(block, "seq", 2 << level) for level, block in enumerate(late)]


def per_device(resident, arriving, gain, triple, exit_matrix, lookup):
    first_in = resident[0]
    me = lax.axis_index("seq")
    levels = jnp.arange(8, dtype=jnp.int32)
    partner = jnp.bitwise_xor(me, jnp.left_shift(1, levels % LEVELS))
    wanted = jnp.broadcast_to(lookup[partner, levels % LEVELS][:, None], (8, 128))
    _, chosen = choose(wanted, first_in, first_in)
    if lax.axis_size("seq") == 16:
        triple, started, far_started, latest, fars = gathered(triple[0], chosen, first_in, gain)
    else:
        triple = lax.all_gather(triple[0], "seq", axis=0, tiled=True)
        fars = partner_rows(chosen)
        started = ahead(triple, [first_in], gain, 0)
        far_started = ahead(triple, fars, gain, HEADS * HEAD)
        latest = []
    first_out = first_layer(far_started, first_in, started, fars, gain, exit_matrix[0], latest)
    moved = from_behind(first_out, "section", 1)
    second_in, chosen = choose(wanted, moved, arriving)
    fars = partner_rows(chosen)
    return second_layer(triple, second_in, ahead(triple, [second_in, fars[0]], gain, 0), fars, gain, exit_matrix[0], latest, first_out)[:, None]


def solution(mesh):
    placed = (
        P("section", "seq", None),
        P("seq", None),
        P("section", None),
        P("section", "seq", None),
        P("section", None, None),
        P(),
    )
    return jax.shard_map(
        per_device,
        mesh=mesh,
        in_specs=placed,
        out_specs=P(None, "section", "seq", None),
        check_vma=False,
    )
```
